128 devices in a mesh: seq: 8 (over y_hi, z), res: 16 (over y_lo, x, core).
Axes of the slice: x: 4, y: 4 (y_hi: 2, y_lo: 2; y = y_hi * 2 + y_lo), z: 4, core: 2. Of those that a mesh axis runs over, the one named last changes fastest.
Arguments:
- homolog_stack: bfloat16 [384, 512, 256], P('seq', 'res'), may hold values from -64 to 64
- entry_exists_flags: int32 [384, 512], P('seq', 'res'), may hold values from 0 to 1, as said below
- genuine_amino_flags: int32 [512], replicated, may hold values 0 or 1
- couplings_tensor: bfloat16 [512, 512, 128], P('res', 'seq'), may hold values from -1.5 to 1.5
- product_source_weights: bfloat16 [256, 32], replicated, may hold values from -0.375 to 0.375
- product_target_weights: bfloat16 [256, 32], replicated, may hold values from -0.375 to 0.375
- product_final_weights: bfloat16 [1024, 128], replicated, may hold values from -0.5625 to 0.5625
- coupling_logit_offset: bfloat16 [128, 8], replicated, may hold values from -1.1953125 to 1.1953125
- horizontal_asking_weights: bfloat16 [256, 256], replicated, may hold values from -0.6 to 0.6
- horizontal_lookup_weights: bfloat16 [256, 256], replicated, may hold values from -0.6 to 0.6
- horizontal_content_weights: bfloat16 [256, 256], replicated, may hold values from -0.375 to 0.375
- horizontal_sigmoid_weights: bfloat16 [256, 256], replicated, may hold values from -0.375 to 0.375
- horizontal_final_weights: bfloat16 [256, 256], replicated, may hold values from -1.5 to 1.5
- vertical_asking_weights: bfloat16 [256, 256], replicated, may hold values from -0.6 to 0.6
- vertical_lookup_weights: bfloat16 [256, 256], replicated, may hold values from -0.6 to 0.6
- vertical_content_weights: bfloat16 [256, 256], replicated, may hold values from -0.375 to 0.375
- vertical_sigmoid_weights: bfloat16 [256, 256], replicated, may hold values from -0.375 to 0.375
- vertical_final_weights: bfloat16 [256, 256], replicated, may hold values from -1.5 to 1.5
Outputs:
- alignment_output: bfloat16 [384, 512, 256], P('seq', 'res')
- pair_output: bfloat16 [512, 512, 128], P('res', 'seq')
The draws below stay inside these ranges and needn't reach their ends.
Inputs may be any that keep to these rules, and one draw needn't show every extreme that they name: `entry_exists_flags`: sequence 0 is present at every residue; every other sequence is present on exactly one contiguous run of residues.
All inputs are finite; a program needn't handle non-finite values.
Results may differ from the reference program's by a relative error of at most 0.02.
Values may be sent and summed in bfloat16 or wider, within the bound.
No kernel may reach another device: no remote copies, remote signals or barrier semaphores. Data moves between devices by JAX's collectives and lax.ppermute only.
A program may use at most 128 MiB of HBM per device.

```python
import math
import jax
import jax.numpy as jnp
from jax import lax

ALIGNMENT_WIDTH = 256
PAIR_CH = 128
ATTENTION_HEADS = 8
HEAD_SIZE = 32
OUTER_CHANNELS = 32
SEQUENCE_COUNT = 384
RESIDUE_COUNT = 512


def drawn_weight(key):
    sampled_values = jax.random.normal(key, (ALIGNMENT_WIDTH, ATTENTION_HEADS * HEAD_SIZE), jnp.float32) / jnp.sqrt(jnp.float32(ALIGNMENT_WIDTH))
    return jnp.clip(sampled_values, -0.59, 0.59)


def subfamily_field(sequence_factors, loading_key):
    loadings = jax.random.normal(loading_key, (4, RESIDUE_COUNT, ALIGNMENT_WIDTH), jnp.float32)
    total = jnp.zeros((SEQUENCE_COUNT, RESIDUE_COUNT, ALIGNMENT_WIDTH), jnp.float32)
    for factor_index in range(4):
        total = total + sequence_factors[:, factor_index][:, None, None] * loadings[factor_index][None]
    return total


def draw_homolog_stack(key, part):
    key = jax.random.fold_in(key, 11)
    first_operand = jax.random.fold_in(key, 0)
    second_operand = jax.random.fold_in(key, 1)
    fifth = jax.random.fold_in(key, 4)
    sixth = jax.random.fold_in(key, 5)
    residue_profile = jax.random.normal(first_operand, (1, RESIDUE_COUNT, ALIGNMENT_WIDTH), jnp.float32)
    sequence_factors = jax.random.normal(fifth, (SEQUENCE_COUNT, 4), jnp.float32)
    random_noise = jax.random.normal(second_operand, (SEQUENCE_COUNT, RESIDUE_COUNT, ALIGNMENT_WIDTH), jnp.float32)
    sampled_values = residue_profile + 0.6 * subfamily_field(sequence_factors, sixth) + random_noise
    return jnp.clip(sampled_values, -64.0, 64.0).astype(jnp.bfloat16)


def draw_entry_exists_flags(key, part):
    key = jax.random.fold_in(key, 12)
    length_key, start_key = jax.random.split(key)
    run_lengths = jax.random.randint(length_key, (SEQUENCE_COUNT,), RESIDUE_COUNT // 4, RESIDUE_COUNT + 1)
    run_starts = jax.random.randint(start_key, (SEQUENCE_COUNT,), 0, RESIDUE_COUNT - run_lengths + 1)
    positions = jnp.arange(RESIDUE_COUNT, dtype=jnp.int32)[None, :]
    present = ((positions >= run_starts[:, None]) & (positions < (run_starts + run_lengths)[:, None])).astype(jnp.int32)
    return present.at[0].set(1)


def draw_horizontal_asking_weights(key, part):
    key = jax.random.fold_in(key, 21)
    weight = drawn_weight(key)
    return weight.astype(jnp.bfloat16)


def draw_horizontal_lookup_weights(key, part):
    key = jax.random.fold_in(key, 22)
    weight = drawn_weight(key)
    return weight.astype(jnp.bfloat16)


def draw_vertical_asking_weights(key, part):
    key = jax.random.fold_in(key, 23)
    weight = drawn_weight(key)
    return weight.astype(jnp.bfloat16)


def draw_vertical_lookup_weights(key, part):
    key = jax.random.fold_in(key, 24)
    weight = drawn_weight(key)
    return weight.astype(jnp.bfloat16)


def touch_ends(values, stream_key, low, top_value):
    longest = values.shape.index(max(values.shape))
    spots = []
    for shift in (0, 1):
        where = [jax.random.randint(jax.random.fold_in(stream_key, axis), (), 0, length) for axis, length in enumerate(values.shape)]
        where[longest] = (where[longest] + shift) % values.shape[longest]
        spots.append(tuple(where))
    return values.at[spots[0]].set(low).at[spots[1]].set(top_value)


def levels(rng, extent, cuts, least, high):
    level = 1.0
    for position, blocks in cuts:
        draws = jax.random.uniform(jax.random.fold_in(jax.random.fold_in(rng, 6), position), (blocks,), jnp.float32, least / len(cuts), high / len(cuts))
        level = level * jnp.repeat(jnp.exp(draws), extent[position] // blocks).reshape((-1,) + (1,) * (len(extent) - 1 - position))
    return level


def scatter_about(rng, shape, scale, limit, pieces=(), kind=jnp.bfloat16):
    factor_of = levels(rng, shape, pieces, -0.22, 0.18) if pieces else 1.0
    result = jax.random.normal(rng, shape, jnp.float32) * scale * factor_of
    return jnp.minimum(jnp.maximum(result, -limit), limit).astype(kind)


def setup_inputs(seed: int = 0) -> dict:
    streams_of = jax.random.split(jax.random.key(seed), 19)
    return {
        "homolog_stack": draw_homolog_stack(jax.random.fold_in(streams_of[18], 71), 0),
        "entry_exists_flags": draw_entry_exists_flags(jax.random.fold_in(streams_of[18], 71), 0),
        "genuine_amino_flags": touch_ends((jax.random.randint(streams_of[2], (RESIDUE_COUNT,), 0, 8) < 7).astype(jnp.int32), jax.random.fold_in(streams_of[2], 1), 0, 1),
        "couplings_tensor": scatter_about(streams_of[3], (RESIDUE_COUNT, RESIDUE_COUNT, PAIR_CH), 0.25, 1.5, ((0, 16), (1, 8))),
        "product_source_weights": scatter_about(streams_of[4], (ALIGNMENT_WIDTH, OUTER_CHANNELS), ALIGNMENT_WIDTH ** -0.5, 0.375),
        "product_target_weights": scatter_about(streams_of[5], (ALIGNMENT_WIDTH, OUTER_CHANNELS), ALIGNMENT_WIDTH ** -0.5, 0.375),
        "product_final_weights": scatter_about(streams_of[6], (OUTER_CHANNELS * OUTER_CHANNELS, PAIR_CH), (3 * (OUTER_CHANNELS * OUTER_CHANNELS) ** -0.5), 0.5625),
        "coupling_logit_offset": scatter_about(streams_of[7], (PAIR_CH, ATTENTION_HEADS), 0.2, 1.1953125),
        "horizontal_asking_weights": draw_horizontal_asking_weights(jax.random.fold_in(streams_of[18], 71), 0),
        "horizontal_lookup_weights": draw_horizontal_lookup_weights(jax.random.fold_in(streams_of[18], 71), 0),
        "horizontal_content_weights": scatter_about(streams_of[10], (ALIGNMENT_WIDTH, ATTENTION_HEADS * HEAD_SIZE), ALIGNMENT_WIDTH ** -0.5, 0.375),
        "horizontal_sigmoid_weights": scatter_about(streams_of[11], (ALIGNMENT_WIDTH, ATTENTION_HEADS * HEAD_SIZE), ALIGNMENT_WIDTH ** -0.5, 0.375),
        "horizontal_final_weights": scatter_about(streams_of[12], (ATTENTION_HEADS * HEAD_SIZE, ALIGNMENT_WIDTH), 0.25, 1.5),
        "vertical_asking_weights": draw_vertical_asking_weights(jax.random.fold_in(streams_of[18], 71), 0),
        "vertical_lookup_weights": draw_vertical_lookup_weights(jax.random.fold_in(streams_of[18], 71), 0),
        "vertical_content_weights": scatter_about(streams_of[15], (ALIGNMENT_WIDTH, ATTENTION_HEADS * HEAD_SIZE), ALIGNMENT_WIDTH ** -0.5, 0.375),
        "vertical_sigmoid_weights": scatter_about(streams_of[16], (ALIGNMENT_WIDTH, ATTENTION_HEADS * HEAD_SIZE), ALIGNMENT_WIDTH ** -0.5, 0.375),
        "vertical_final_weights": scatter_about(streams_of[17], (ATTENTION_HEADS * HEAD_SIZE, ALIGNMENT_WIDTH), 0.25, 1.5),
    }


def standardize_features(sampled_values):
    sampled_values = sampled_values.astype(jnp.float32)
    center = sampled_values - lax.optimization_barrier(jnp.mean(sampled_values, axis=-1, keepdims=True))
    spread = lax.optimization_barrier(jnp.mean(center * center, axis=-1, keepdims=True))
    return center * lax.rsqrt(spread + 1e-05)

def linear_project(sampled_values, weight):
    return jnp.dot(sampled_values, weight, preferred_element_type=jnp.float32)

def softmax_last(scores):
    top = lax.optimization_barrier(jnp.max(scores, axis=-1, keepdims=True))
    expo = jnp.exp(scores - top)
    return expo / lax.optimization_barrier(jnp.sum(expo, axis=-1, keepdims=True))

def reference(homolog_stack, entry_exists_flags, genuine_amino_flags, couplings_tensor, product_source_weights, product_target_weights, product_final_weights, coupling_logit_offset, horizontal_asking_weights, horizontal_lookup_weights, horizontal_content_weights, horizontal_sigmoid_weights, horizontal_final_weights, vertical_asking_weights, vertical_lookup_weights, vertical_content_weights, vertical_sigmoid_weights, vertical_final_weights):
    mask_float = entry_exists_flags.astype(jnp.float32)
    rmask = genuine_amino_flags.astype(jnp.float32)
    score_scale = HEAD_SIZE ** (-0.5)
    standardized_homologs = standardize_features(homolog_stack).astype(jnp.bfloat16)
    left_projected = (linear_project(standardized_homologs, product_source_weights) * mask_float[..., None]).astype(jnp.bfloat16)
    right_projected = (linear_project(standardized_homologs, product_target_weights) * mask_float[..., None]).astype(jnp.bfloat16)
    block = math.gcd(RESIDUE_COUNT, 32)
    final_cube = product_final_weights.astype(jnp.float32).reshape(OUTER_CHANNELS, OUTER_CHANNELS, PAIR_CH)
    right_float = right_projected.astype(jnp.float32)

    def opm_rows(block_index):
        left_rows = lax.dynamic_slice_in_dim(left_projected, block_index * block, block, 1).astype(jnp.float32)
        folded_left = jnp.einsum('sic,cdo->sido', left_rows, final_cube).astype(jnp.bfloat16)
        return jnp.einsum('sido,sjd->ijo', folded_left.astype(jnp.float32), right_float)
    opm_sum = lax.map(opm_rows, jnp.arange(RESIDUE_COUNT // block, dtype=jnp.int32))
    opm_sum = opm_sum.reshape(RESIDUE_COUNT, RESIDUE_COUNT, PAIR_CH)
    pair_count = jnp.dot(mask_float.T, mask_float, precision=lax.Precision.HIGHEST)
    factor = rmask[:, None] * rmask[None, :] / (pair_count + 0.001)
    pair_output = (couplings_tensor.astype(jnp.float32) + factor[..., None] * opm_sum).astype(jnp.bfloat16)
    ln_pair = standardize_features(pair_output).astype(jnp.bfloat16)
    pair_bias = jnp.transpose(linear_project(ln_pair, coupling_logit_offset).astype(jnp.bfloat16), (2, 0, 1))
    bias_f = pair_bias.astype(jnp.float32)
    row_query_heads = (linear_project(standardized_homologs, horizontal_asking_weights) * score_scale).astype(jnp.bfloat16)
    row_key_heads = linear_project(standardized_homologs, horizontal_lookup_weights).astype(jnp.bfloat16)
    row_value_heads = linear_project(standardized_homologs, horizontal_content_weights).astype(jnp.bfloat16)
    row_gate_values = jax.nn.sigmoid(linear_project(standardized_homologs, horizontal_sigmoid_weights))

    def row_one(seq_pick):
        queries = row_query_heads[seq_pick].astype(jnp.float32).reshape(RESIDUE_COUNT, ATTENTION_HEADS, HEAD_SIZE)
        keyset = row_key_heads[seq_pick].astype(jnp.float32).reshape(RESIDUE_COUNT, ATTENTION_HEADS, HEAD_SIZE)
        valueset = row_value_heads[seq_pick].astype(jnp.float32).reshape(RESIDUE_COUNT, ATTENTION_HEADS, HEAD_SIZE)
        scores = jnp.einsum('ihd,jhd->hij', queries, keyset) + bias_f
        scores = jnp.where(mask_float[seq_pick][None, None, :] > 0, scores, -1000000000.0)
        weights = softmax_last(scores)
        return jnp.einsum('hij,jhd->ihd', weights, valueset).reshape(RESIDUE_COUNT, ATTENTION_HEADS * HEAD_SIZE)
    row_attended = lax.map(row_one, jnp.arange(SEQUENCE_COUNT, dtype=jnp.int32))
    row_gated = (row_gate_values * row_attended).astype(jnp.bfloat16)
    horizontal_increment = linear_project(row_gated, horizontal_final_weights).astype(jnp.bfloat16)
    homolog_intermediate = (homolog_stack.astype(jnp.float32) + horizontal_increment.astype(jnp.float32)).astype(jnp.bfloat16)
    normalized_middle = standardize_features(homolog_intermediate).astype(jnp.bfloat16)
    col_query = (linear_project(normalized_middle, vertical_asking_weights) * score_scale).astype(jnp.bfloat16)
    col_key = linear_project(normalized_middle, vertical_lookup_weights).astype(jnp.bfloat16)
    col_value = linear_project(normalized_middle, vertical_content_weights).astype(jnp.bfloat16)
    col_gate = jax.nn.sigmoid(linear_project(normalized_middle, vertical_sigmoid_weights))

    def col_one(res_pick):
        queries = lax.dynamic_index_in_dim(col_query, res_pick, 1, False).astype(jnp.float32).reshape(SEQUENCE_COUNT, ATTENTION_HEADS, HEAD_SIZE)
        keyset = lax.dynamic_index_in_dim(col_key, res_pick, 1, False).astype(jnp.float32).reshape(SEQUENCE_COUNT, ATTENTION_HEADS, HEAD_SIZE)
        valueset = lax.dynamic_index_in_dim(col_value, res_pick, 1, False).astype(jnp.float32).reshape(SEQUENCE_COUNT, ATTENTION_HEADS, HEAD_SIZE)
        column_mask = lax.dynamic_index_in_dim(mask_float, res_pick, 1, False)
        scores = jnp.einsum('shd,thd->hst', queries, keyset)
        scores = jnp.where(column_mask[None, None, :] > 0, scores, -1000000000.0)
        weights = softmax_last(scores)
        return jnp.einsum('hst,thd->shd', weights, valueset).reshape(SEQUENCE_COUNT, ATTENTION_HEADS * HEAD_SIZE)
    col_attended = jnp.transpose(lax.map(col_one, jnp.arange(RESIDUE_COUNT, dtype=jnp.int32)), (1, 0, 2))
    col_gated = (col_gate * col_attended).astype(jnp.bfloat16)
    column_delta = linear_project(col_gated, vertical_final_weights).astype(jnp.bfloat16)
    alignment_output = (homolog_intermediate.astype(jnp.float32) + column_delta.astype(jnp.float32)).astype(jnp.bfloat16)
    return (alignment_output, pair_output)
```

```python
import math

import jax
import jax.numpy as jnp
from jax import lax
from jax.experimental import pallas as pl
from jax.experimental.pallas import tpu as pltpu
from jax.sharding import Mesh
from jax.sharding import PartitionSpec as P

HEADS = 8
HEAD = 32
F32 = jnp.float32
BF16 = jnp.bfloat16
NEG = -1e9
STEP = 3
PICK = 2
SEQ = ("yh", "z")
RES = ("yl", "xh", "xl", "core")
ALL = SEQ + RES
TEAM = ("yl", "xh")
PLANE = SEQ + TEAM
NT = (((1,), (1,)), ((), ()))
TN = (((0,), (0,)), ((), ()))
VMEM_LIMIT = 24 * 1024 * 1024
LOG2E = math.log2(math.e)


def normalize(values):
    values = values.astype(F32)
    center = values - jnp.mean(values, axis=-1, keepdims=True)
    spread = jnp.mean(center * center, axis=-1, keepdims=True)
    return (center * lax.rsqrt(spread + 1e-5)).astype(BF16)


def project(values, weight):
    return jnp.dot(values, weight, preferred_element_type=F32)


class Attention:
    def __init__(self, query_t, key, value_t, bias_of, mask_lanes, lane):
        self.query_t, self.key, self.value_t = query_t, key, value_t
        self.bias_of, self.mask_lanes, self.lane = bias_of, mask_lanes, lane
        self.count = query_t.shape[1]
        self.found = []

    def score(self, pair):
        part = slice(pair // 2 * 128, pair // 2 * 128 + 128)
        own = self.query_t[part]
        row = lax.broadcasted_iota(jnp.int32, own.shape, 0)
        one = jnp.where(row == self.lane, 1.0, 0.0).astype(BF16)
        stacked = []
        for h in range(2):
            mine = row // HEAD == pair % 2 * 2 + h
            stacked.append(jnp.concatenate([jnp.where(mine, own, jnp.zeros_like(own)), one], axis=0))
        keys = jnp.concatenate([self.key[:, part], self.mask_lanes], axis=1)
        return project(keys, jnp.concatenate(stacked, axis=1))

    def weigh(self, pair, scores):
        weights = []
        for h in range(2):
            extra = self.bias_of(pair * 2 + h)
            for low in range(0, self.count, 128):
                tile = scores[:, h * self.count + low : h * self.count + low + 128]
                if extra is not None:
                    tile = tile + extra[:, low : low + 128]
                weights.append(jnp.exp2(tile - jnp.max(tile, axis=0, keepdims=True)).astype(BF16))
        return jnp.concatenate(weights, axis=1)

    def mix(self, pair, weights):
        ones = jnp.ones((16, self.value_t.shape[1]), BF16)
        values = jnp.concatenate([self.value_t[pair * 64 : pair * 64 + 64], ones], axis=0)
        mixed = project(values, weights)
        for h in range(2):
            cols = slice(h * self.count, (h + 1) * self.count)
            self.found.append(mixed[h * HEAD : (h + 1) * HEAD, cols] / mixed[64:65, cols])

    def result(self):
        return jnp.concatenate(self.found, axis=0)


def run_pipelined(attentions, finish):
    units = [(a, pair) for a in attentions for pair in range(4)]
    ahead = units[0][0].score(0)
    for place, (attention, pair) in enumerate(units):
        scores = ahead
        if place + 1 < len(units):
            ahead = units[place + 1][0].score(units[place + 1][1])
        attention.mix(pair, attention.weigh(pair, scores))
        if pair == 3:
            finish(attentions.index(attention), attention.result())


def mask_columns(mask_row):
    shape = (128, mask_row.shape[1])
    top = lax.broadcasted_iota(jnp.int32, shape, 0) == 0
    return jnp.where(top, jnp.broadcast_to(mask_row, shape), 0.0).astype(BF16).T


def factor_kernel(x_ref, mask_ref, source_ref, target_ref, left_ref, right_ref, lefts, rights):
    ln = normalize(x_ref[...].reshape(1536, 256))
    mask = mask_ref[...].astype(F32).T
    lefts[:, :32] = lax.dot_general(ln, source_ref[...], NT, preferred_element_type=F32)
    turned = lax.dot_general(target_ref[...], ln, NT, preferred_element_type=F32)
    for s in range(48):
        rights[s * 32 : (s + 1) * 32, :32] = turned[:, s * 32 : (s + 1) * 32]
    wide = jnp.concatenate([mask] * 4, axis=1)
    for tile in range(8):
        lanes = slice(tile * 128, (tile + 1) * 128)
        spots = [pl.ds(tile * 4 + e, 48, stride=32) for e in range(4)]
        parts = [lefts[spot, :][:, :32] for spot in spots]
        parts = [p * mask[:, tile * 4 + e : tile * 4 + e + 1] for e, p in enumerate(parts)]
        left_ref[:, lanes] = jnp.concatenate(parts, axis=1).astype(BF16)
        parts = [rights[spot, :][:, :32] for spot in spots]
        right_ref[:, lanes] = (jnp.concatenate(parts, axis=1) * wide).astype(BF16)
    tail = jnp.concatenate([mask, jnp.zeros((48, 96), F32)], axis=1).astype(BF16)
    left_ref[:, 1024:] = tail
    right_ref[:, 1024:] = tail


def pair_kernel(at_ref, *refs):
    left_pieces = refs[:4]
    mine_ref, other_ref, pair_ref, rows_ref, cols_ref, final_ref, offset_ref = refs[4:11]
    out_ref, bias_ref, column_ref, left_hold, right_hold, hold = refs[11:]
    seq_at, core = at_ref[0], at_ref[1]
    right_hold[core] = mine_ref[...]
    right_hold[1 - core] = other_ref[...]
    for k in range(8):
        left_hold[seq_at ^ k] = left_pieces[k % 4][k // 4]
    left_all = left_hold[...].reshape(384, 1152)
    right = [right_hold[p].reshape(384, 1152) for p in range(2)]
    left_mask = left_all[:, 1024:1056]
    picks = lax.broadcasted_iota(jnp.int32, (8, 32), 0) + seq_at * 4
    picks = (picks == lax.broadcasted_iota(jnp.int32, (8, 32), 1)).astype(BF16)
    present = lax.dot_general(picks, left_mask, NT, preferred_element_type=F32)
    column_ref[...] = (present - 1.0) * -NEG
    count = jnp.concatenate(
        [
            lax.dot_general(r[:, 1024:1056], left_mask, TN, preferred_element_type=F32)
            for r in right
        ],
        axis=0,
    )
    factor = cols_ref[...] * rows_ref[...] / (count + 0.001)
    offset = offset_ref[...]
    def outer_of(block):
        left = left_all[:, block * 256 : (block + 1) * 256]
        return [
            lax.dot_general(left, r[:, :1024], TN, preferred_element_type=F32).astype(BF16)
            for r in right
        ]

    ahead = outer_of(0)
    for block in range(4):
        outer = ahead
        if block < 3:
            ahead = outer_of(block + 1)
        turned = []
        for i in range(8):
            for p in range(2):
                rows = outer[p][i * 32 : (i + 1) * 32]
                tiles = [rows[:, t * 128 : (t + 1) * 128] for t in range(8)]
                turned.append(jnp.concatenate(tiles, axis=0).T)
        terms = None
        for e in range(4):
            lhs = jnp.concatenate([t[e * 32 : (e + 1) * 32] for t in turned], axis=0)
            part = project(lhs, final_ref[e])
            terms = part if terms is None else terms + part
        for i in range(8):
            at = block * 8 + i
            sums = terms[i * 64 : (i + 1) * 64]
            fresh = pair_ref[at].astype(F32) + factor[:, at : at + 1] * sums
            fresh = fresh.astype(BF16)
            out_ref[at] = fresh
            bias = lax.dot_general(offset, normalize(fresh), NT, preferred_element_type=F32)
            hold[:, at : at + 1, :] = bias[:, None, :]
    for h in range(8):
        turned = hold[h].T
        quarters = [turned[q * 16 : (q + 1) * 16] for q in range(4)]
        block = jnp.concatenate(quarters, axis=1).astype(BF16)
        for reader in range(32):
            bias_ref[reader, h] = block


def ready_kernel(at_ref, *refs):
    x_ref, xc_ref, xx_ref, xxc_ref = refs[:4]
    tails = refs[4:8]
    wq_ref, wk_ref, wv_ref, wg_ref = refs[8:12]
    query_ref, key_ref, value_ref, gate_ref, mask_ref, ordered, columns = refs[12:]
    xl, core = at_ref[0], at_ref[1]

    @pl.when(pl.program_id(0) == 0)
    def _():
        columns[...] = jnp.zeros_like(columns)
        places = [(xl, core), (xl, 1 - core), (1 - xl, core), (1 - xl, 1 - core)]
        for tail_ref, (a, b) in zip(tails, places):
            for u in range(4):
                absent = ((tail_ref[u, :, :128].astype(F32) - 1.0) * -NEG).T
                columns[u, a, b, :, :16] = absent[:32]
        mask_ref[...] = columns[...].reshape(512, 128).astype(BF16)

    for t in range(STEP):
        rows = slice(t * 32, (t + 1) * 32)
        asked = normalize(x_ref[:, rows].reshape(128, 256))
        ordered[t, :, xl, core] = asked.reshape(4, 32, 256)
        ordered[t, :, xl, 1 - core] = normalize(xc_ref[:, rows])
        ordered[t, :, 1 - xl, core] = normalize(xx_ref[:, rows])
        ordered[t, :, 1 - xl, 1 - core] = normalize(xxc_ref[:, rows])
        keys = ordered[t].reshape(512, 256)
        query_ref[t] = (project(asked, wq_ref[...]) * (HEAD**-0.5 * LOG2E)).T.astype(BF16)
        key_ref[t] = project(keys, wk_ref[...]).astype(BF16)
        value_ref[t] = project(keys, wv_ref[...]).astype(BF16).T
        gate_ref[t] = jax.nn.sigmoid(project(asked, wg_ref[...])).T


def row_kernel(
    x_ref, query_ref, key_ref, value_ref, gate_ref, mask_ref, bias_ref, wo_ref, out_ref, held
):
    @pl.when(pl.program_id(0) == 0)
    def _():
        for a in range(8):
            for j in range(4):
                low = a * 64 + j * 16
                parts = [bias_ref[a, q, :, :, j * 32 : (j + 1) * 32] for q in range(4)]
                part = jnp.concatenate(parts, axis=2).astype(F32)
                held[:, low : low + 16] = part * LOG2E

    def finish(t, found):
        gated = (gate_ref[t] * found).astype(BF16)
        update = lax.dot_general(gated, wo_ref[...], TN, preferred_element_type=F32).astype(BF16)
        raw = x_ref[:, t * 32 : (t + 1) * 32].reshape(128, 256)
        out_ref[t] = (raw.astype(F32) + update.astype(F32)).astype(BF16)

    attentions = [
        Attention(
            query_ref[t],
            key_ref[t],
            value_ref[t],
            lambda h: held[h],
            mask_ref[...],
            pl.program_id(0) * STEP + t,
        )
        for t in range(STEP)
    ]
    run_pipelined(attentions, finish)


def column_kernel(x_ref, mask_ref, wq_ref, wk_ref, wv_ref, wg_ref, wo_ref, out_ref):
    gates, attentions = [], []
    for r in range(PICK):
        keys = normalize(x_ref[r])
        keys_t = keys.T

        def turned(weight_ref):
            return lax.dot_general(weight_ref[...], keys_t, TN, preferred_element_type=F32)

        query_t = (turned(wq_ref) * (HEAD**-0.5 * LOG2E)).astype(BF16)
        key = project(keys, wk_ref[...]).astype(BF16)
        value_t = turned(wv_ref).astype(BF16)
        gates.append(jax.nn.sigmoid(turned(wg_ref)))
        mask = mask_columns(mask_ref[pl.ds(pl.program_id(0) * PICK + r, 1), :])
        attentions.append(Attention(query_t, key, value_t, lambda h: None, mask, 0))

    def finish(r, found):
        gated = (gates[r] * found).astype(BF16)
        update = lax.dot_general(gated, wo_ref[...], TN, preferred_element_type=F32).astype(BF16)
        out_ref[r] = (x_ref[r].astype(F32) + update.astype(F32)).astype(BF16)

    run_pipelined(attentions, finish)


def in_hbm(array):
    return pltpu.with_memory_space_constraint(array, pltpu.HBM)


def spread(block, axes, count):
    wide = jnp.broadcast_to(block[None], (count,) + block.shape)
    return lax.all_to_all(wide, axes, split_axis=0, concat_axis=0, tiled=True)


def whole(shape):
    zeros = (0,) * len(shape)
    return pl.BlockSpec(shape, lambda *_: zeros)


def body(
    homolog_stack,
    entry_exists_flags,
    genuine_amino_flags,
    couplings_tensor,
    product_source_weights,
    product_target_weights,
    product_final_weights,
    coupling_logit_offset,
    horizontal_asking_weights,
    horizontal_lookup_weights,
    horizontal_content_weights,
    horizontal_sigmoid_weights,
    horizontal_final_weights,
    vertical_asking_weights,
    vertical_lookup_weights,
    vertical_content_weights,
    vertical_sigmoid_weights,
    vertical_final_weights,
):
    seq_at = lax.axis_index(SEQ)
    res_at = lax.axis_index(RES)
    xl_at = lax.axis_index("xl")
    core_at = lax.axis_index("core")
    mask = entry_exists_flags.astype(BF16)

    left, right = pl.pallas_call(
        factor_kernel,
        out_shape=[jax.ShapeDtypeStruct((48, 1152), BF16)] * 2,
        scratch_shapes=[pltpu.VMEM((1536, 128), F32)] * 2,
        compiler_params=pltpu.CompilerParams(vmem_limit_bytes=VMEM_LIMIT),
        name="factors",
    )(
        in_hbm(homolog_stack),
        in_hbm(entry_exists_flags.T),
        in_hbm(product_source_weights.T),
        in_hbm(product_target_weights.T),
    )
    swap = [
        ((a * 8 + b) * 2 + p, (b * 8 + a) * 2 + p)
        for a in range(8)
        for b in range(8)
        for p in range(2)
    ]
    pairs = [(0, 1), (1, 0)]
    right = lax.ppermute(right, ALL, swap)
    left_yh = lax.ppermute(left, "yh", pairs)
    right, left_yh = lax.optimization_barrier((right, left_yh))
    mine = spread(right, ("yl", "xh", "xl"), 8)
    left = jnp.stack([left, left_yh])
    lefts = [left] + [
        lax.ppermute(left, "z", [(z, z ^ k) for z in range(4)]) for k in range(1, 4)
    ]
    homolog_stack, mask, lefts[1] = lax.optimization_barrier((homolog_stack, mask, lefts[1]))
    tail = jnp.pad(mask.reshape(4, 12, 32), ((0, 0), (0, 4), (0, 224)))
    packed = jnp.concatenate([homolog_stack.reshape(4, 384, 256), tail], axis=1)
    team_at = lax.axis_index(TEAM)
    parts = []
    for k in range(4):
        part = lax.dynamic_index_in_dim(packed, team_at ^ k, 0, False)
        parts.append(lax.ppermute(part, TEAM, [(t, t ^ k) for t in range(4)]) if k else part)
    packed = jnp.stack(parts).reshape(2, 2, 400, 256)
    packed = jnp.where(lax.axis_index("yl") == 1, packed[::-1], packed)
    packed = jnp.where(lax.axis_index("xh") == 1, packed[:, ::-1], packed)
    packed = packed.reshape(4, 400, 256)
    final = product_final_weights.reshape(32, 8, 4, 128)
    final = jnp.transpose(final, (2, 1, 0, 3)).reshape(4, 256, 128)
    mine, final, packed, *lefts = lax.optimization_barrier((mine, final, packed, *lefts))
    other = lax.ppermute(mine, "core", pairs)
    packed_x = lax.ppermute(packed, "xl", pairs)
    packed_c = lax.ppermute(packed, "core", pairs)

    flags = genuine_amino_flags.astype(F32)
    row_flags = lax.dynamic_slice_in_dim(flags, res_at * 32, 32).reshape(1, 32)
    col_flags = lax.dynamic_slice_in_dim(flags, seq_at * 64, 64).reshape(64, 1)
    square = whole((256, 256))
    smem = pl.BlockSpec(memory_space=pltpu.SMEM)
    vmem = pl.BlockSpec(memory_space=pltpu.VMEM)
    pair_output, bias, col_mask = pl.pallas_call(
        pair_kernel,
        out_shape=(
            jax.ShapeDtypeStruct((32, 64, 128), BF16),
            jax.ShapeDtypeStruct((32, 8, 16, 128), BF16),
            jax.ShapeDtypeStruct((8, 384), F32),
        ),
        in_specs=[smem] + [vmem] * 11,
        scratch_shapes=[
            pltpu.VMEM((8, 48, 1152), BF16),
            pltpu.VMEM((2, 8, 48, 1152), BF16),
            pltpu.VMEM((8, 32, 64), F32),
        ],
        compiler_params=pltpu.CompilerParams(vmem_limit_bytes=VMEM_LIMIT),
        cost_estimate=pl.CostEstimate(
            flops=1000, transcendentals=0, bytes_accessed=1000
        ),
        name="pair",
    )(
        jnp.stack([seq_at, core_at]).astype(jnp.int32),
        *lefts,
        mine,
        other,
        couplings_tensor,
        row_flags,
        col_flags,
        final,
        coupling_logit_offset.T,
    )

    packed, packed_c, packed_x, _ = lax.optimization_barrier((packed, packed_c, packed_x, bias))
    packed_xc = lax.ppermute(packed_x, "core", pairs)
    pieces = [in_hbm(p) for p in (packed, packed_c, packed_x, packed_xc)]
    by_row = [(12, 256, 128), (12, 512, 256), (12, 256, 512), (12, 256, 128)]
    specs = [pl.BlockSpec((STEP,) + shape[1:], lambda t: (t, 0, 0)) for shape in by_row]
    rows_in = pl.pallas_call(
        ready_kernel,
        out_shape=[
            pltpu.HBM(shape, kind)
            for shape, kind in zip(by_row, (BF16, BF16, BF16, F32))
        ]
        + [pltpu.HBM((512, 128), BF16)],
        grid=(12 // STEP,),
        in_specs=[smem] + [pl.BlockSpec((4, STEP * 32, 256), lambda t: (0, t, 0))] * 4
        + [pl.BlockSpec((4, 16, 256), lambda t: (0, 24, 0))] * 4
        + [square] * 4,
        out_specs=specs + [whole((512, 128))],
        scratch_shapes=[
            pltpu.VMEM((STEP, 4, 2, 2, 32, 256), BF16),
            pltpu.VMEM((4, 2, 2, 32, 128), F32),
        ],
        compiler_params=pltpu.CompilerParams(vmem_limit_bytes=VMEM_LIMIT),
        cost_estimate=pl.CostEstimate(flops=1000, transcendentals=0, bytes_accessed=1000),
        name="ready",
    )(
        jnp.stack([xl_at, core_at]).astype(jnp.int32),
        *pieces,
        *pieces,
        in_hbm(horizontal_asking_weights),
        in_hbm(horizontal_lookup_weights),
        in_hbm(horizontal_content_weights),
        in_hbm(horizontal_sigmoid_weights),
    )
    bias = lax.all_to_all(bias, PLANE, split_axis=0, concat_axis=0, tiled=True)
    bias = bias.reshape(8, 4, 8, 16, 128)

    rows_in = [in_hbm(a) for a in rows_in]
    middle = pl.pallas_call(
        row_kernel,
        out_shape=jax.ShapeDtypeStruct((12, 128, 256), BF16),
        grid=(12 // STEP,),
        in_specs=[pl.BlockSpec((4, STEP * 32, 256), lambda t: (0, t, 0))]
        + specs
        + [whole((512, 128)), whole((8, 4, 8, 16, 128)), square],
        out_specs=pl.BlockSpec((STEP, 128, 256), lambda t: (t, 0, 0)),
        scratch_shapes=[pltpu.VMEM((8, 512, 128), F32)],
        compiler_params=pltpu.CompilerParams(vmem_limit_bytes=VMEM_LIMIT),
        cost_estimate=pl.CostEstimate(
            flops=8_000_000_000, transcendentals=6_300_000, bytes_accessed=12_000_000
        ),
        name="rows",
    )(pieces[0], *rows_in, bias, horizontal_final_weights)

    middle = jnp.transpose(middle.reshape(12, 4, 8, 4, 256), (2, 1, 0, 3, 4))
    middle = lax.all_to_all(
        middle.reshape(32, 12, 4, 256), PLANE, split_axis=0, concat_axis=0, tiled=True
    )
    middle = jnp.transpose(middle.reshape(384, 4, 256), (1, 0, 2))
    columns = pl.pallas_call(
        column_kernel,
        out_shape=jax.ShapeDtypeStruct((4, 384, 256), BF16),
        grid=(4 // PICK,),
        in_specs=[
            pl.BlockSpec((PICK, 384, 256), lambda r: (r, 0, 0)),
            whole((8, 384)),
            square,
            square,
            square,
            square,
            square,
        ],
        out_specs=pl.BlockSpec((PICK, 384, 256), lambda r: (r, 0, 0)),
        compiler_params=pltpu.CompilerParams(vmem_limit_bytes=VMEM_LIMIT),
        cost_estimate=pl.CostEstimate(
            flops=8_000_000_000, transcendentals=4_700_000, bytes_accessed=2_000_000
        ),
        name="columns",
    )(
        middle,
        col_mask,
        vertical_asking_weights,
        vertical_lookup_weights,
        vertical_content_weights,
        vertical_sigmoid_weights,
        vertical_final_weights,
    )
    columns = jnp.transpose(columns.reshape(4, 8, 48, 256), (1, 0, 2, 3))
    columns = lax.all_to_all(columns, SEQ, split_axis=0, concat_axis=0, tiled=True)
    alignment_output = jnp.transpose(columns.reshape(32, 48, 256), (1, 0, 2))
    return alignment_output, pair_output


def solution(mesh):
    parts = Mesh(mesh.devices.reshape(2, 4, 2, 2, 2, 2), ALL)
    stack = P(SEQ, RES, None)
    in_specs = (stack, P(SEQ, RES), P(), P(RES, SEQ, None)) + (P(),) * 14
    out_specs = (stack, P(RES, SEQ, None))
    return jax.shard_map(body, mesh=parts, in_specs=in_specs, out_specs=out_specs, check_vma=False)
```

```python
import math

import jax
import jax.numpy as jnp
from jax import lax
from jax.experimental import pallas as pl
from jax.experimental.pallas import tpu as pltpu
from jax.sharding import Mesh
from jax.sharding import PartitionSpec as P

HEADS = 8
HEAD = 32
F32 = jnp.float32
BF16 = jnp.bfloat16
NEG = -1e9
STEP = 3
PICK = 2
SEQ = ("yh", "z")
RES = ("yl", "xh", "xl", "core")
ALL = SEQ + RES
TEAM = ("yl", "xh")
PLANE = SEQ + TEAM
NT = (((1,), (1,)), ((), ()))
TN = (((0,), (0,)), ((), ()))
VMEM_LIMIT = 24 * 1024 * 1024
LOG2E = math.log2(math.e)


def normalize(values):
    values = values.astype(F32)
    center = values - jnp.mean(values, axis=-1, keepdims=True)
    spread = jnp.mean(center * center, axis=-1, keepdims=True)
    return (center * lax.rsqrt(spread + 1e-5)).astype(BF16)


def project(values, weight):
    return jnp.dot(values, weight, preferred_element_type=F32)


class Attention:
    def __init__(self, query_t, key, value_t, bias_of, mask_lanes, lane, heads):
        self.query_t, self.key, self.value_t = query_t, key, value_t
        self.bias_of, self.mask_lanes, self.lane = bias_of, mask_lanes, lane
        self.heads = heads
        self.units = HEADS // heads
        self.count = query_t.shape[1]
        self.found = []

    def score(self, unit):
        first = unit * self.heads
        part = slice(first // 4 * 128, first // 4 * 128 + 128)
        own = self.query_t[part]
        row = lax.broadcasted_iota(jnp.int32, own.shape, 0)
        one = jnp.where(row == self.lane, 1.0, 0.0).astype(BF16)
        stacked = []
        for h in range(self.heads):
            mine = row // HEAD == first % 4 + h
            stacked.append(jnp.concatenate([jnp.where(mine, own, jnp.zeros_like(own)), one], axis=0))
        keys = jnp.concatenate([self.key[:, part], self.mask_lanes], axis=1)
        return project(keys, jnp.concatenate(stacked, axis=1))

    def weigh(self, unit, scores):
        weights = []
        for h in range(self.heads):
            extra = self.bias_of(unit * self.heads + h)
            for low in range(0, self.count, 128):
                tile = scores[:, h * self.count + low : h * self.count + low + 128]
                if extra is not None:
                    tile = tile + extra[:, low : low + 128]
                weights.append(jnp.exp2(tile - jnp.max(tile, axis=0, keepdims=True)).astype(BF16))
        return jnp.concatenate(weights, axis=1)

    def mix(self, unit, weights):
        size = self.heads * HEAD
        ones = jnp.ones((16, self.value_t.shape[1]), BF16)
        values = jnp.concatenate([self.value_t[unit * size : (unit + 1) * size], ones], axis=0)
        mixed = project(values, weights)
        for h in range(self.heads):
            cols = slice(h * self.count, (h + 1) * self.count)
            self.found.append(mixed[h * HEAD : (h + 1) * HEAD, cols] / mixed[size : size + 1, cols])

    def result(self):
        return jnp.concatenate(self.found, axis=0)


def run_pipelined(attentions, finish):
    units = [(a, unit) for a in attentions for unit in range(a.units)]
    ahead = units[0][0].score(0)
    for place, (attention, unit) in enumerate(units):
        scores = ahead
        if place + 1 < len(units):
            ahead = units[place + 1][0].score(units[place + 1][1])
        attention.mix(unit, attention.weigh(unit, scores))
        if unit == attention.units - 1:
            finish(attentions.index(attention), attention.result())


def mask_columns(mask_row):
    shape = (128, mask_row.shape[1])
    top = lax.broadcasted_iota(jnp.int32, shape, 0) == 0
    return jnp.where(top, jnp.broadcast_to(mask_row, shape), 0.0).astype(BF16).T


def factor_kernel(
    x_ref, mask_ref, source_ref, target_ref, left_ref, right_ref, packed_ref, lefts, rights
):
    ln = normalize(x_ref[...].reshape(1536, 256))
    mask = mask_ref[...].astype(F32).T
    lefts[:, :32] = lax.dot_general(ln, source_ref[...], NT, preferred_element_type=F32)
    turned = lax.dot_general(target_ref[...], ln, NT, preferred_element_type=F32)
    for s in range(48):
        rights[s * 32 : (s + 1) * 32, :32] = turned[:, s * 32 : (s + 1) * 32]
    wide = jnp.concatenate([mask] * 4, axis=1)
    for tile in range(8):
        lanes = slice(tile * 128, (tile + 1) * 128)
        spots = [pl.ds(tile * 4 + e, 48, stride=32) for e in range(4)]
        parts = [lefts[spot, :][:, :32] for spot in spots]
        parts = [p * mask[:, tile * 4 + e : tile * 4 + e + 1] for e, p in enumerate(parts)]
        left_ref[:, lanes] = jnp.concatenate(parts, axis=1).astype(BF16)
        parts = [rights[spot, :][:, :32] for spot in spots]
        right_ref[:, lanes] = (jnp.concatenate(parts, axis=1) * wide).astype(BF16)
    tail = jnp.concatenate([mask, jnp.zeros((48, 96), F32)], axis=1).astype(BF16)
    left_ref[:, 1024:] = tail
    right_ref[:, 1024:] = tail
    for u in range(4):
        packed_ref[u, :384] = x_ref[u * 12 : (u + 1) * 12].reshape(384, 256)
        flags = jnp.concatenate([mask[u * 12 : (u + 1) * 12], jnp.zeros((4, 32), F32)], axis=0)
        flags = jnp.concatenate([flags, jnp.zeros((16, 224), F32)], axis=1)
        packed_ref[u, 384:] = flags.astype(BF16)


def pair_kernel(at_ref, *refs):
    left_pieces = refs[:4]
    mine_ref, other_ref, pair_ref, rows_ref, cols_ref, final_ref, offset_ref = refs[4:11]
    out_ref, bias_ref, column_ref, left_hold, right_hold, hold = refs[11:]
    seq_at, core = at_ref[0], at_ref[1]
    for k in range(8):
        place = k // 4 * 4 + (k + 8 - seq_at) % 4
        right_hold[core, place] = mine_ref[k]
        right_hold[1 - core, place] = other_ref[k]
    for k in range(8):
        left_hold[seq_at ^ k] = left_pieces[k % 4][k // 4]
    left_all = left_hold[...].reshape(384, 1152)
    right = [right_hold[p].reshape(384, 1152) for p in range(2)]
    left_mask = left_all[:, 1024:1056]
    picks = lax.broadcasted_iota(jnp.int32, (8, 32), 0) + seq_at * 4
    picks = (picks == lax.broadcasted_iota(jnp.int32, (8, 32), 1)).astype(BF16)
    present = lax.dot_general(picks, left_mask, NT, preferred_element_type=F32)
    column_ref[...] = (present - 1.0) * -NEG
    count = jnp.concatenate(
        [
            lax.dot_general(r[:, 1024:1056], left_mask, TN, preferred_element_type=F32)
            for r in right
        ],
        axis=0,
    )
    factor = cols_ref[...] * rows_ref[...] / (count + 0.001)
    offset = offset_ref[...]
    def outer_of(block):
        left = left_all[:, block * 512 : (block + 1) * 512]
        return [
            lax.dot_general(left, r[:, :1024], TN, preferred_element_type=F32).astype(BF16)
            for r in right
        ]

    ahead = outer_of(0)
    for block in range(2):
        outer = ahead
        if block < 1:
            ahead = outer_of(block + 1)
        turned = []
        for i in range(16):
            for p in range(2):
                rows = outer[p][i * 32 : (i + 1) * 32]
                tiles = [rows[:, t * 128 : (t + 1) * 128] for t in range(8)]
                turned.append(jnp.concatenate(tiles, axis=0).T)
        terms = None
        for e in range(4):
            lhs = jnp.concatenate([t[e * 32 : (e + 1) * 32] for t in turned], axis=0)
            part = project(lhs, final_ref[e])
            terms = part if terms is None else terms + part
        for i in range(16):
            at = block * 16 + i
            sums = terms[i * 64 : (i + 1) * 64]
            fresh = pair_ref[at].astype(F32) + factor[:, at : at + 1] * sums
            fresh = fresh.astype(BF16)
            out_ref[at] = fresh
            bias = lax.dot_general(offset, normalize(fresh), NT, preferred_element_type=F32)
            hold[:, at : at + 1, :] = bias[:, None, :]
    for h in range(8):
        turned = hold[h].T
        quarters = [turned[q * 16 : (q + 1) * 16] for q in range(4)]
        block = jnp.concatenate(quarters, axis=1).astype(BF16)
        for reader in range(32):
            bias_ref[reader, h] = block


def ready_kernel(at_ref, *refs):
    x_ref, xc_ref, xx_ref, xxc_ref = refs[:4]
    tails = refs[4:8]
    wq_ref, wk_ref, wv_ref, wg_ref = refs[8:12]
    query_ref, key_ref, value_ref, gate_ref, mask_ref, ordered, columns = refs[12:]
    xl, core = at_ref[0], at_ref[1]

    @pl.when(pl.program_id(0) == 0)
    def _():
        columns[...] = jnp.zeros_like(columns)
        places = [(xl, core), (xl, 1 - core), (1 - xl, core), (1 - xl, 1 - core)]
        for tail_ref, (a, b) in zip(tails, places):
            for u in range(4):
                absent = ((tail_ref[u, :, :128].astype(F32) - 1.0) * -NEG).T
                columns[u, a, b, :, :16] = absent[:32]
        mask_ref[...] = columns[...].reshape(512, 128).astype(BF16)

    for t in range(STEP):
        rows = slice(t * 32, (t + 1) * 32)
        asked = normalize(x_ref[:, rows].reshape(128, 256))
        ordered[t, :, xl, core] = asked.reshape(4, 32, 256)
        ordered[t, :, xl, 1 - core] = normalize(xc_ref[:, rows])
        ordered[t, :, 1 - xl, core] = normalize(xx_ref[:, rows])
        ordered[t, :, 1 - xl, 1 - core] = normalize(xxc_ref[:, rows])
        keys = ordered[t].reshape(512, 256)
        query_ref[t] = (project(asked, wq_ref[...]) * (HEAD**-0.5 * LOG2E)).T.astype(BF16)
        key_ref[t] = project(keys, wk_ref[...]).astype(BF16)
        value_ref[t] = project(keys, wv_ref[...]).astype(BF16).T
        gate_ref[t] = jax.nn.sigmoid(project(asked, wg_ref[...])).T


def row_kernel(
    x_ref, query_ref, key_ref, value_ref, gate_ref, mask_ref, bias_ref, wo_ref, out_ref, held
):
    @pl.when(pl.program_id(0) == 0)
    def _():
        for a in range(8):
            for j in range(4):
                low = a * 64 + j * 16
                parts = [bias_ref[a, q, :, :, j * 32 : (j + 1) * 32] for q in range(4)]
                part = jnp.concatenate(parts, axis=2).astype(F32)
                held[:, low : low + 16] = part * LOG2E

    def finish(t, found):
        gated = (gate_ref[t] * found).astype(BF16)
        update = lax.dot_general(gated, wo_ref[...], TN, preferred_element_type=F32).astype(BF16)
        raw = x_ref[:, t * 32 : (t + 1) * 32].reshape(128, 256)
        out_ref[t] = (raw.astype(F32) + update.astype(F32)).astype(BF16)

    attentions = [
        Attention(
            query_ref[t],
            key_ref[t],
            value_ref[t],
            lambda h: held[h],
            mask_ref[...],
            pl.program_id(0) * STEP + t,
            4,
        )
        for t in range(STEP)
    ]
    run_pipelined(attentions, finish)


def column_kernel(x_ref, mask_ref, wq_ref, wk_ref, wv_ref, wg_ref, wo_ref, out_ref):
    gates, attentions = [], []
    for r in range(PICK):
        keys = normalize(x_ref[r])
        keys_t = keys.T

        def turned(weight_ref):
            return lax.dot_general(weight_ref[...], keys_t, TN, preferred_element_type=F32)

        query_t = (turned(wq_ref) * (HEAD**-0.5 * LOG2E)).astype(BF16)
        key = project(keys, wk_ref[...]).astype(BF16)
        value_t = turned(wv_ref).astype(BF16)
        gates.append(jax.nn.sigmoid(turned(wg_ref)))
        mask = mask_columns(mask_ref[pl.ds(pl.program_id(0) * PICK + r, 1), :])
        attentions.append(Attention(query_t, key, value_t, lambda h: None, mask, 0, 2))

    def finish(r, found):
        gated = (gates[r] * found).astype(BF16)
        update = lax.dot_general(gated, wo_ref[...], TN, preferred_element_type=F32).astype(BF16)
        out_ref[r] = (x_ref[r].astype(F32) + update.astype(F32)).astype(BF16)

    run_pipelined(attentions, finish)


def in_hbm(array):
    return pltpu.with_memory_space_constraint(array, pltpu.HBM)


def spread(block, axes, count):
    wide = jnp.broadcast_to(block[None], (count,) + block.shape)
    return lax.all_to_all(wide, axes, split_axis=0, concat_axis=0, tiled=True)


def whole(shape):
    zeros = (0,) * len(shape)
    return pl.BlockSpec(shape, lambda *_: zeros)


def body(
    homolog_stack,
    entry_exists_flags,
    genuine_amino_flags,
    couplings_tensor,
    product_source_weights,
    product_target_weights,
    product_final_weights,
    coupling_logit_offset,
    horizontal_asking_weights,
    horizontal_lookup_weights,
    horizontal_content_weights,
    horizontal_sigmoid_weights,
    horizontal_final_weights,
    vertical_asking_weights,
    vertical_lookup_weights,
    vertical_content_weights,
    vertical_sigmoid_weights,
    vertical_final_weights,
):
    seq_at = lax.axis_index(SEQ)
    res_at = lax.axis_index(RES)
    xl_at = lax.axis_index("xl")
    core_at = lax.axis_index("core")

    left, right, packed = pl.pallas_call(
        factor_kernel,
        out_shape=[jax.ShapeDtypeStruct((48, 1152), BF16)] * 2
        + [jax.ShapeDtypeStruct((4, 400, 256), BF16)],
        scratch_shapes=[pltpu.VMEM((1536, 128), F32)] * 2,
        compiler_params=pltpu.CompilerParams(vmem_limit_bytes=VMEM_LIMIT),
        name="factors",
    )(
        in_hbm(homolog_stack),
        in_hbm(entry_exists_flags.T),
        in_hbm(product_source_weights.T),
        in_hbm(product_target_weights.T),
    )
    swap = [
        ((a * 8 + b) * 2 + p, (b * 8 + a // 4 * 4 + (a + b) % 4) * 2 + p)
        for a in range(8)
        for b in range(8)
        for p in range(2)
    ]
    pairs = [(0, 1), (1, 0)]
    right = lax.ppermute(right, ALL, swap)
    left_yh = lax.ppermute(left, "yh", pairs)
    team_at = lax.axis_index(TEAM)
    parts = []
    for k in range(4):
        part = lax.dynamic_index_in_dim(packed, team_at ^ k, 0, False)
        parts.append(lax.ppermute(part, TEAM, [(t, t ^ k) for t in range(4)]) if k else part)
    right, left_yh, parts[2] = lax.optimization_barrier((right, left_yh, parts[2]))
    packed = jnp.stack(parts).reshape(2, 2, 400, 256)
    packed = jnp.where(lax.axis_index("yl") == 1, packed[::-1], packed)
    packed = jnp.where(lax.axis_index("xh") == 1, packed[:, ::-1], packed)
    packed = packed.reshape(4, 400, 256)
    mine = spread(right, ("yl", "xh", "xl"), 8)
    left = jnp.stack([left, left_yh])
    lefts = [left] + [
        lax.ppermute(left, "z", [(z, z ^ k) for z in range(4)]) for k in range(1, 4)
    ]
    final = product_final_weights.reshape(32, 8, 4, 128)
    final = jnp.transpose(final, (2, 1, 0, 3)).reshape(4, 256, 128)
    mine, final, *lefts = lax.optimization_barrier((mine, final, *lefts))
    other = lax.ppermute(mine, "core", pairs)
    packed_x = lax.ppermute(packed, "xl", pairs)
    packed_c = lax.ppermute(packed, "core", pairs)

    flags = genuine_amino_flags.astype(F32)
    row_flags = lax.dynamic_slice_in_dim(flags, res_at * 32, 32).reshape(1, 32)
    col_flags = lax.dynamic_slice_in_dim(flags, seq_at * 64, 64).reshape(64, 1)
    square = whole((256, 256))
    smem = pl.BlockSpec(memory_space=pltpu.SMEM)
    vmem = pl.BlockSpec(memory_space=pltpu.VMEM)
    pair_output, bias, col_mask = pl.pallas_call(
        pair_kernel,
        out_shape=(
            jax.ShapeDtypeStruct((32, 64, 128), BF16),
            jax.ShapeDtypeStruct((32, 8, 16, 128), BF16),
            jax.ShapeDtypeStruct((8, 384), F32),
        ),
        in_specs=[smem] + [vmem] * 11,
        scratch_shapes=[
            pltpu.VMEM((8, 48, 1152), BF16),
            pltpu.VMEM((2, 8, 48, 1152), BF16),
            pltpu.VMEM((8, 32, 64), F32),
        ],
        compiler_params=pltpu.CompilerParams(vmem_limit_bytes=VMEM_LIMIT),
        cost_estimate=pl.CostEstimate(
            flops=1000, transcendentals=0, bytes_accessed=1000
        ),
        name="pair",
    )(
        jnp.stack([seq_at, core_at]).astype(jnp.int32),
        *lefts,
        mine,
        other,
        couplings_tensor,
        row_flags,
        col_flags,
        final,
        coupling_logit_offset.T,
    )

    packed, packed_c, packed_x, _ = lax.optimization_barrier((packed, packed_c, packed_x, bias))
    packed_xc = lax.ppermute(packed_x, "core", pairs)
    pieces = [in_hbm(p) for p in (packed, packed_c, packed_x, packed_xc)]
    by_row = [(12, 256, 128), (12, 512, 256), (12, 256, 512), (12, 256, 128)]
    specs = [pl.BlockSpec((STEP,) + shape[1:], lambda t: (t, 0, 0)) for shape in by_row]
    rows_in = pl.pallas_call(
        ready_kernel,
        out_shape=[
            pltpu.HBM(shape, kind)
            for shape, kind in zip(by_row, (BF16, BF16, BF16, F32))
        ]
        + [pltpu.HBM((512, 128), BF16)],
        grid=(12 // STEP,),
        in_specs=[smem] + [pl.BlockSpec((4, STEP * 32, 256), lambda t: (0, t, 0))] * 4
        + [pl.BlockSpec((4, 16, 256), lambda t: (0, 24, 0))] * 4
        + [square] * 4,
        out_specs=specs + [whole((512, 128))],
        scratch_shapes=[
            pltpu.VMEM((STEP, 4, 2, 2, 32, 256), BF16),
            pltpu.VMEM((4, 2, 2, 32, 128), F32),
        ],
        compiler_params=pltpu.CompilerParams(vmem_limit_bytes=VMEM_LIMIT),
        cost_estimate=pl.CostEstimate(flops=1000, transcendentals=0, bytes_accessed=1000),
        name="ready",
    )(
        jnp.stack([xl_at, core_at]).astype(jnp.int32),
        *pieces,
        *pieces,
        in_hbm(horizontal_asking_weights),
        in_hbm(horizontal_lookup_weights),
        in_hbm(horizontal_content_weights),
        in_hbm(horizontal_sigmoid_weights),
    )
    bias = lax.all_to_all(bias, PLANE, split_axis=0, concat_axis=0, tiled=True)
    bias = bias.reshape(8, 4, 8, 16, 128)

    rows_in = [in_hbm(a) for a in rows_in]
    middle = pl.pallas_call(
        row_kernel,
        out_shape=jax.ShapeDtypeStruct((12, 128, 256), BF16),
        grid=(12 // STEP,),
        in_specs=[pl.BlockSpec((4, STEP * 32, 256), lambda t: (0, t, 0))]
        + specs
        + [whole((512, 128)), whole((8, 4, 8, 16, 128)), square],
        out_specs=pl.BlockSpec((STEP, 128, 256), lambda t: (t, 0, 0)),
        scratch_shapes=[pltpu.VMEM((8, 512, 128), F32)],
        compiler_params=pltpu.CompilerParams(vmem_limit_bytes=VMEM_LIMIT),
        cost_estimate=pl.CostEstimate(
            flops=8_000_000_000, transcendentals=6_300_000, bytes_accessed=12_000_000
        ),
        name="rows",
    )(pieces[0], *rows_in, bias, horizontal_final_weights)

    middle = jnp.transpose(middle.reshape(12, 4, 8, 4, 256), (2, 1, 0, 3, 4))
    middle = lax.all_to_all(
        middle.reshape(32, 12, 4, 256), PLANE, split_axis=0, concat_axis=0, tiled=True
    )
    middle = jnp.transpose(middle.reshape(384, 4, 256), (1, 0, 2))
    columns = pl.pallas_call(
        column_kernel,
        out_shape=jax.ShapeDtypeStruct((4, 384, 256), BF16),
        grid=(4 // PICK,),
        in_specs=[
            pl.BlockSpec((PICK, 384, 256), lambda r: (r, 0, 0)),
            whole((8, 384)),
            square,
            square,
            square,
            square,
            square,
        ],
        out_specs=pl.BlockSpec((PICK, 384, 256), lambda r: (r, 0, 0)),
        compiler_params=pltpu.CompilerParams(vmem_limit_bytes=VMEM_LIMIT),
        cost_estimate=pl.CostEstimate(
            flops=8_000_000_000, transcendentals=4_700_000, bytes_accessed=2_000_000
        ),
        name="columns",
    )(
        middle,
        col_mask,
        vertical_asking_weights,
        vertical_lookup_weights,
        vertical_content_weights,
        vertical_sigmoid_weights,
        vertical_final_weights,
    )
    columns = jnp.transpose(columns.reshape(4, 8, 48, 256), (1, 0, 2, 3))
    columns = lax.all_to_all(columns, SEQ, split_axis=0, concat_axis=0, tiled=True)
    alignment_output = jnp.transpose(columns.reshape(32, 48, 256), (1, 0, 2))
    return alignment_output, pair_output


def solution(mesh):
    parts = Mesh(mesh.devices.reshape(2, 4, 2, 2, 2, 2), ALL)
    stack = P(SEQ, RES, None)
    in_specs = (stack, P(SEQ, RES), P(), P(RES, SEQ, None)) + (P(),) * 14
    out_specs = (stack, P(RES, SEQ, None))
    return jax.shard_map(body, mesh=parts, in_specs=in_specs, out_specs=out_specs, check_vma=False)
```

```python
import math

import jax
import jax.numpy as jnp
from jax import lax
from jax.experimental import pallas as pl
from jax.experimental.pallas import tpu as pltpu
from jax.sharding import Mesh
from jax.sharding import PartitionSpec as P

HEADS = 8
HEAD = 32
F32 = jnp.float32
BF16 = jnp.bfloat16
NEG = -1e9
STEP = 3
PICK = 2
SEQ = ("yh", "z")
RES = ("yl", "xh", "xl", "core")
ALL = SEQ + RES
TEAM = ("yl", "xh")
PLANE = SEQ + TEAM
NT = (((1,), (1,)), ((), ()))
TN = (((0,), (0,)), ((), ()))
VMEM_LIMIT = 24 * 1024 * 1024
LOG2E = math.log2(math.e)


def normalize(values):
    values = values.astype(F32)
    center = values - jnp.mean(values, axis=-1, keepdims=True)
    spread = jnp.mean(center * center, axis=-1, keepdims=True)
    return (center * lax.rsqrt(spread + 1e-5)).astype(BF16)


def project(values, weight):
    return jnp.dot(values, weight, preferred_element_type=F32)


class Attention:
    def __init__(self, query_t, key, value_t, bias_of, mask_lanes, lane, heads):
        self.query_t, self.key, self.value_t = query_t, key, value_t
        self.bias_of, self.mask_lanes, self.lane = bias_of, mask_lanes, lane
        self.heads = heads
        self.units = HEADS // heads
        self.count = query_t.shape[1]
        self.found = []

    def score(self, unit):
        first = unit * self.heads
        part = slice(first // 4 * 128, first // 4 * 128 + 128)
        own = self.query_t[part]
        row = lax.broadcasted_iota(jnp.int32, own.shape, 0)
        one = jnp.where(row == self.lane, 1.0, 0.0).astype(BF16)
        stacked = []
        for h in range(self.heads):
            mine = row // HEAD == first % 4 + h
            stacked.append(jnp.concatenate([jnp.where(mine, own, jnp.zeros_like(own)), one], axis=0))
        keys = jnp.concatenate([self.key[:, part], self.mask_lanes], axis=1)
        return project(keys, jnp.concatenate(stacked, axis=1))

    def weigh(self, unit, scores):
        weights = []
        for h in range(self.heads):
            extra = self.bias_of(unit * self.heads + h)
            for low in range(0, self.count, 128):
                tile = scores[:, h * self.count + low : h * self.count + low + 128]
                if extra is not None:
                    tile = tile + extra[:, low : low + 128]
                weights.append(jnp.exp2(tile - jnp.max(tile, axis=0, keepdims=True)).astype(BF16))
        return jnp.concatenate(weights, axis=1)

    def mix(self, unit, weights):
        size = self.heads * HEAD
        ones = jnp.ones((16, self.value_t.shape[1]), BF16)
        values = jnp.concatenate([self.value_t[unit * size : (unit + 1) * size], ones], axis=0)
        mixed = project(values, weights)
        for h in range(self.heads):
            cols = slice(h * self.count, (h + 1) * self.count)
            self.found.append(mixed[h * HEAD : (h + 1) * HEAD, cols] / mixed[size : size + 1, cols])

    def result(self):
        return jnp.concatenate(self.found, axis=0)


def run_pipelined(attentions, finish):
    units = [(a, unit) for a in attentions for unit in range(a.units)]
    ahead = units[0][0].score(0)
    for place, (attention, unit) in enumerate(units):
        scores = ahead
        if place + 1 < len(units):
            ahead = units[place + 1][0].score(units[place + 1][1])
        attention.mix(unit, attention.weigh(unit, scores))
        if unit == attention.units - 1:
            finish(attentions.index(attention), attention.result())


def mask_columns(mask_row):
    shape = (128, mask_row.shape[1])
    top = lax.broadcasted_iota(jnp.int32, shape, 0) == 0
    return jnp.where(top, jnp.broadcast_to(mask_row, shape), 0.0).astype(BF16).T


def factor_kernel(
    x_ref, mask_ref, source_ref, target_ref, left_ref, right_ref, packed_ref, lefts, rights
):
    ln = normalize(x_ref[...].reshape(1536, 256))
    mask = mask_ref[...].astype(F32).T
    lefts[:, :32] = lax.dot_general(ln, source_ref[...], NT, preferred_element_type=F32)
    turned = lax.dot_general(target_ref[...], ln, NT, preferred_element_type=F32)
    for s in range(48):
        rights[s * 32 : (s + 1) * 32, :32] = turned[:, s * 32 : (s + 1) * 32]
    wide = jnp.concatenate([mask] * 4, axis=1)
    for tile in range(8):
        lanes = slice(tile * 128, (tile + 1) * 128)
        spots = [pl.ds(tile * 4 + e, 48, stride=32) for e in range(4)]
        parts = [lefts[spot, :][:, :32] for spot in spots]
        parts = [p * mask[:, tile * 4 + e : tile * 4 + e + 1] for e, p in enumerate(parts)]
        left_ref[:, lanes] = jnp.concatenate(parts, axis=1).astype(BF16)
        parts = [rights[spot, :][:, :32] for spot in spots]
        right_ref[:, lanes] = (jnp.concatenate(parts, axis=1) * wide).astype(BF16)
    tail = jnp.concatenate([mask, jnp.zeros((48, 96), F32)], axis=1).astype(BF16)
    left_ref[:, 1024:] = tail
    right_ref[:, 1024:] = tail
    for u in range(4):
        packed_ref[u, :384] = x_ref[u * 12 : (u + 1) * 12].reshape(384, 256)
        flags = jnp.concatenate([mask[u * 12 : (u + 1) * 12], jnp.zeros((4, 32), F32)], axis=0)
        flags = jnp.concatenate([flags, jnp.zeros((16, 224), F32)], axis=1)
        packed_ref[u, 384:] = flags.astype(BF16)


def pair_kernel(at_ref, *refs):
    left_pieces = refs[:4]
    mine_ref, other_ref, pair_ref, rows_ref, cols_ref, final_ref, offset_ref = refs[4:11]
    out_ref, bias_ref, column_ref, left_hold, right_hold, hold = refs[11:]
    seq_at, core = at_ref[0], at_ref[1]
    for k in range(8):
        place = k // 4 * 4 + (k + 8 - seq_at) % 4
        right_hold[core, place] = mine_ref[k]
        right_hold[1 - core, place] = other_ref[k]
    for k in range(8):
        left_hold[seq_at ^ k] = left_pieces[k % 4][k // 4]
    left_all = left_hold[...].reshape(384, 1152)
    right = [right_hold[p].reshape(384, 1152) for p in range(2)]
    left_mask = left_all[:, 1024:1056]
    picks = lax.broadcasted_iota(jnp.int32, (8, 32), 0) + seq_at * 4
    picks = (picks == lax.broadcasted_iota(jnp.int32, (8, 32), 1)).astype(BF16)
    present = lax.dot_general(picks, left_mask, NT, preferred_element_type=F32)
    column_ref[...] = (present - 1.0) * -NEG
    count = jnp.concatenate(
        [
            lax.dot_general(r[:, 1024:1056], left_mask, TN, preferred_element_type=F32)
            for r in right
        ],
        axis=0,
    )
    factor = cols_ref[...] * rows_ref[...] / (count + 0.001)
    offset = offset_ref[...]
    def outer_of(block):
        left = left_all[:, block * 512 : (block + 1) * 512]
        return [
            lax.dot_general(left, r[:, :1024], TN, preferred_element_type=F32).astype(BF16)
            for r in right
        ]

    ahead = outer_of(0)
    for block in range(2):
        outer = ahead
        if block < 1:
            ahead = outer_of(block + 1)
        turned = []
        for i in range(16):
            for p in range(2):
                rows = outer[p][i * 32 : (i + 1) * 32]
                tiles = [rows[:, t * 128 : (t + 1) * 128] for t in range(8)]
                turned.append(jnp.concatenate(tiles, axis=0).T)
        terms = None
        for e in range(4):
            lhs = jnp.concatenate([t[e * 32 : (e + 1) * 32] for t in turned], axis=0)
            part = project(lhs, final_ref[e])
            terms = part if terms is None else terms + part
        for i in range(16):
            at = block * 16 + i
            sums = terms[i * 64 : (i + 1) * 64]
            fresh = pair_ref[at].astype(F32) + factor[:, at : at + 1] * sums
            fresh = fresh.astype(BF16)
            out_ref[at] = fresh
            bias = lax.dot_general(offset, normalize(fresh), NT, preferred_element_type=F32)
            hold[:, at : at + 1, :] = bias[:, None, :]
    for h in range(8):
        turned = hold[h].T
        quarters = [turned[q * 16 : (q + 1) * 16] for q in range(4)]
        block = jnp.concatenate(quarters, axis=1).astype(BF16)
        for reader in range(32):
            bias_ref[reader, h] = block


def ready_kernel(at_ref, *refs):
    x_ref, xc_ref, xx_ref, xxc_ref = refs[:4]
    tails = refs[4:8]
    wq_ref, wk_ref, wv_ref, wg_ref = refs[8:12]
    query_ref, key_ref, value_ref, gate_ref, mask_ref, ordered, columns = refs[12:]
    xl, core = at_ref[0], at_ref[1]

    @pl.when(pl.program_id(0) == 0)
    def _():
        columns[...] = jnp.zeros_like(columns)
        places = [(xl, core), (xl, 1 - core), (1 - xl, core), (1 - xl, 1 - core)]
        for tail_ref, (a, b) in zip(tails, places):
            for u in range(4):
                absent = ((tail_ref[u, :, :128].astype(F32) - 1.0) * -NEG).T
                columns[u, a, b, :, :16] = absent[:32]
        mask_ref[...] = columns[...].reshape(512, 128).astype(BF16)

    asked = []
    for t in range(STEP):
        rows = slice(t * 32, (t + 1) * 32)
        asked.append(normalize(x_ref[:, rows].reshape(128, 256)))
        ordered[t, :, xl, core] = asked[t].reshape(4, 32, 256)
        ordered[t, :, xl, 1 - core] = normalize(xc_ref[:, rows])
        ordered[t, :, 1 - xl, core] = normalize(xx_ref[:, rows])
        ordered[t, :, 1 - xl, 1 - core] = normalize(xxc_ref[:, rows])
    keys = ordered[...].reshape(STEP * 512, 256)
    both = project(keys, jnp.concatenate([wk_ref[...], wv_ref[...]], axis=1))
    asking = jnp.concatenate([wq_ref[...], wg_ref[...]], axis=1)
    asks = project(jnp.concatenate(asked, axis=0), asking)
    for t in range(STEP):
        own = asks[t * 128 : (t + 1) * 128]
        query_ref[t] = (own[:, :256] * (HEAD**-0.5 * LOG2E)).T.astype(BF16)
        gate_ref[t] = jax.nn.sigmoid(own[:, 256:]).T
        rows = slice(t * 512, (t + 1) * 512)
        key_ref[t] = both[rows, :256].astype(BF16)
        value_ref[t] = both[rows, 256:].astype(BF16).T


def row_kernel(
    x_ref, query_ref, key_ref, value_ref, gate_ref, mask_ref, bias_ref, wo_ref, out_ref, held
):
    @pl.when(pl.program_id(0) == 0)
    def _():
        for a in range(8):
            for j in range(4):
                low = a * 64 + j * 16
                parts = [bias_ref[a, q, :, :, j * 32 : (j + 1) * 32] for q in range(4)]
                part = jnp.concatenate(parts, axis=2).astype(F32)
                held[:, low : low + 16] = part * LOG2E

    def finish(t, found):
        gated = (gate_ref[t] * found).astype(BF16)
        update = lax.dot_general(gated, wo_ref[...], TN, preferred_element_type=F32).astype(BF16)
        raw = x_ref[:, t * 32 : (t + 1) * 32].reshape(128, 256)
        out_ref[t] = (raw.astype(F32) + update.astype(F32)).astype(BF16)

    attentions = [
        Attention(
            query_ref[t],
            key_ref[t],
            value_ref[t],
            lambda h: held[h],
            mask_ref[...],
            pl.program_id(0) * STEP + t,
            4,
        )
        for t in range(STEP)
    ]
    run_pipelined(attentions, finish)


def column_kernel(x_ref, mask_ref, wq_ref, wk_ref, wv_ref, wg_ref, wo_ref, out_ref):
    keys = normalize(x_ref[...].reshape(PICK * 384, 256))
    key = project(keys, wk_ref[...]).astype(BF16)
    weights = jnp.concatenate([wq_ref[...], wv_ref[...], wg_ref[...]], axis=1)
    turned = lax.dot_general(weights, keys.T, TN, preferred_element_type=F32)
    query_t = (turned[:256] * (HEAD**-0.5 * LOG2E)).astype(BF16)
    value_t = turned[256:512].astype(BF16)
    gate = jax.nn.sigmoid(turned[512:])
    gates, attentions = [], []
    for r in range(PICK):
        rows = slice(r * 384, (r + 1) * 384)
        gates.append(gate[:, rows])
        mask = mask_columns(mask_ref[pl.ds(pl.program_id(0) * PICK + r, 1), :])
        attentions.append(
            Attention(query_t[:, rows], key[rows], value_t[:, rows], lambda h: None, mask, 0, 2)
        )

    def finish(r, found):
        gated = (gates[r] * found).astype(BF16)
        update = lax.dot_general(gated, wo_ref[...], TN, preferred_element_type=F32).astype(BF16)
        out_ref[r] = (x_ref[r].astype(F32) + update.astype(F32)).astype(BF16)

    run_pipelined(attentions, finish)


def in_hbm(array):
    return pltpu.with_memory_space_constraint(array, pltpu.HBM)


def spread(block, axes, count):
    wide = jnp.broadcast_to(block[None], (count,) + block.shape)
    return lax.all_to_all(wide, axes, split_axis=0, concat_axis=0, tiled=True)


def whole(shape):
    zeros = (0,) * len(shape)
    return pl.BlockSpec(shape, lambda *_: zeros)


def body(
    homolog_stack,
    entry_exists_flags,
    genuine_amino_flags,
    couplings_tensor,
    product_source_weights,
    product_target_weights,
    product_final_weights,
    coupling_logit_offset,
    horizontal_asking_weights,
    horizontal_lookup_weights,
    horizontal_content_weights,
    horizontal_sigmoid_weights,
    horizontal_final_weights,
    vertical_asking_weights,
    vertical_lookup_weights,
    vertical_content_weights,
    vertical_sigmoid_weights,
    vertical_final_weights,
):
    seq_at = lax.axis_index(SEQ)
    res_at = lax.axis_index(RES)
    xl_at = lax.axis_index("xl")
    core_at = lax.axis_index("core")

    left, right, packed = pl.pallas_call(
        factor_kernel,
        out_shape=[jax.ShapeDtypeStruct((48, 1152), BF16)] * 2
        + [jax.ShapeDtypeStruct((4, 400, 256), BF16)],
        scratch_shapes=[pltpu.VMEM((1536, 128), F32)] * 2,
        compiler_params=pltpu.CompilerParams(vmem_limit_bytes=VMEM_LIMIT),
        name="factors",
    )(
        in_hbm(homolog_stack),
        in_hbm(entry_exists_flags.T),
        in_hbm(product_source_weights.T),
        in_hbm(product_target_weights.T),
    )
    swap = [
        ((a * 8 + b) * 2 + p, (b * 8 + a // 4 * 4 + (a + b) % 4) * 2 + p)
        for a in range(8)
        for b in range(8)
        for p in range(2)
    ]
    pairs = [(0, 1), (1, 0)]
    right = lax.ppermute(right, ALL, swap)
    left_yh = lax.ppermute(left, "yh", pairs)
    team_at = lax.axis_index(TEAM)
    parts = []
    for k in range(4):
        part = lax.dynamic_index_in_dim(packed, team_at ^ k, 0, False)
        parts.append(lax.ppermute(part, TEAM, [(t, t ^ k) for t in range(4)]) if k else part)
    packed = jnp.stack(parts).reshape(2, 2, 400, 256)
    packed = jnp.where(lax.axis_index("yl") == 1, packed[::-1], packed)
    packed = jnp.where(lax.axis_index("xh") == 1, packed[:, ::-1], packed)
    packed = packed.reshape(4, 400, 256)
    right, left_yh, packed = lax.optimization_barrier((right, left_yh, packed))
    mine = spread(right, ("yl", "xh", "xl"), 8)
    left = jnp.stack([left, left_yh])
    lefts = [left] + [
        lax.ppermute(left, "z", [(z, z ^ k) for z in range(4)]) for k in range(1, 4)
    ]
    final = product_final_weights.reshape(32, 8, 4, 128)
    final = jnp.transpose(final, (2, 1, 0, 3)).reshape(4, 256, 128)
    mine, final, *lefts = lax.optimization_barrier((mine, final, *lefts))
    other = lax.ppermute(mine, "core", pairs)
    packed_x = lax.ppermute(packed, "xl", pairs)
    packed_c = lax.ppermute(packed, "core", pairs)

    flags = genuine_amino_flags.astype(F32)
    row_flags = lax.dynamic_slice_in_dim(flags, res_at * 32, 32).reshape(1, 32)
    col_flags = lax.dynamic_slice_in_dim(flags, seq_at * 64, 64).reshape(64, 1)
    square = whole((256, 256))
    smem = pl.BlockSpec(memory_space=pltpu.SMEM)
    vmem = pl.BlockSpec(memory_space=pltpu.VMEM)
    pair_output, bias, col_mask = pl.pallas_call(
        pair_kernel,
        out_shape=(
            jax.ShapeDtypeStruct((32, 64, 128), BF16),
            jax.ShapeDtypeStruct((32, 8, 16, 128), BF16),
            jax.ShapeDtypeStruct((8, 384), F32),
        ),
        in_specs=[smem] + [vmem] * 11,
        scratch_shapes=[
            pltpu.VMEM((8, 48, 1152), BF16),
            pltpu.VMEM((2, 8, 48, 1152), BF16),
            pltpu.VMEM((8, 32, 64), F32),
        ],
        compiler_params=pltpu.CompilerParams(vmem_limit_bytes=VMEM_LIMIT),
        cost_estimate=pl.CostEstimate(
            flops=1000, transcendentals=0, bytes_accessed=1000
        ),
        name="pair",
    )(
        jnp.stack([seq_at, core_at]).astype(jnp.int32),
        *lefts,
        mine,
        other,
        couplings_tensor,
        row_flags,
        col_flags,
        final,
        coupling_logit_offset.T,
    )

    packed, packed_c, packed_x, _ = lax.optimization_barrier((packed, packed_c, packed_x, bias))
    packed_xc = lax.ppermute(packed_x, "core", pairs)
    pieces = [in_hbm(p) for p in (packed, packed_c, packed_x, packed_xc)]
    by_row = [(12, 256, 128), (12, 512, 256), (12, 256, 512), (12, 256, 128)]
    specs = [pl.BlockSpec((STEP,) + shape[1:], lambda t: (t, 0, 0)) for shape in by_row]
    rows_in = pl.pallas_call(
        ready_kernel,
        out_shape=[
            pltpu.HBM(shape, kind)
            for shape, kind in zip(by_row, (BF16, BF16, BF16, F32))
        ]
        + [pltpu.HBM((512, 128), BF16)],
        grid=(12 // STEP,),
        in_specs=[smem] + [pl.BlockSpec((4, STEP * 32, 256), lambda t: (0, t, 0))] * 4
        + [pl.BlockSpec((4, 16, 256), lambda t: (0, 24, 0))] * 4
        + [square] * 4,
        out_specs=specs + [whole((512, 128))],
        scratch_shapes=[
            pltpu.VMEM((STEP, 4, 2, 2, 32, 256), BF16),
            pltpu.VMEM((4, 2, 2, 32, 128), F32),
        ],
        compiler_params=pltpu.CompilerParams(vmem_limit_bytes=VMEM_LIMIT),
        cost_estimate=pl.CostEstimate(flops=1000, transcendentals=0, bytes_accessed=1000),
        name="ready",
    )(
        jnp.stack([xl_at, core_at]).astype(jnp.int32),
        *pieces,
        *pieces,
        in_hbm(horizontal_asking_weights),
        in_hbm(horizontal_lookup_weights),
        in_hbm(horizontal_content_weights),
        in_hbm(horizontal_sigmoid_weights),
    )
    bias = lax.all_to_all(bias, PLANE, split_axis=0, concat_axis=0, tiled=True)
    bias = bias.reshape(8, 4, 8, 16, 128)

    rows_in = [in_hbm(a) for a in rows_in]
    middle = pl.pallas_call(
        row_kernel,
        out_shape=jax.ShapeDtypeStruct((12, 128, 256), BF16),
        grid=(12 // STEP,),
        in_specs=[pl.BlockSpec((4, STEP * 32, 256), lambda t: (0, t, 0))]
        + specs
        + [whole((512, 128)), whole((8, 4, 8, 16, 128)), square],
        out_specs=pl.BlockSpec((STEP, 128, 256), lambda t: (t, 0, 0)),
        scratch_shapes=[pltpu.VMEM((8, 512, 128), F32)],
        compiler_params=pltpu.CompilerParams(vmem_limit_bytes=VMEM_LIMIT),
        cost_estimate=pl.CostEstimate(
            flops=8_000_000_000, transcendentals=6_300_000, bytes_accessed=12_000_000
        ),
        name="rows",
    )(pieces[0], *rows_in, bias, horizontal_final_weights)

    middle = jnp.transpose(middle.reshape(12, 4, 8, 4, 256), (2, 1, 0, 3, 4))
    middle = lax.all_to_all(
        middle.reshape(32, 12, 4, 256), PLANE, split_axis=0, concat_axis=0, tiled=True
    )
    middle = jnp.transpose(middle.reshape(384, 4, 256), (1, 0, 2))
    columns = pl.pallas_call(
        column_kernel,
        out_shape=jax.ShapeDtypeStruct((4, 384, 256), BF16),
        grid=(4 // PICK,),
        in_specs=[
            pl.BlockSpec((PICK, 384, 256), lambda r: (r, 0, 0)),
            whole((8, 384)),
            square,
            square,
            square,
            square,
            square,
        ],
        out_specs=pl.BlockSpec((PICK, 384, 256), lambda r: (r, 0, 0)),
        compiler_params=pltpu.CompilerParams(vmem_limit_bytes=VMEM_LIMIT),
        cost_estimate=pl.CostEstimate(
            flops=8_000_000_000, transcendentals=4_700_000, bytes_accessed=2_000_000
        ),
        name="columns",
    )(
        middle,
        col_mask,
        vertical_asking_weights,
        vertical_lookup_weights,
        vertical_content_weights,
        vertical_sigmoid_weights,
        vertical_final_weights,
    )
    columns = jnp.transpose(columns.reshape(4, 8, 48, 256), (1, 0, 2, 3))
    columns = lax.all_to_all(columns, SEQ, split_axis=0, concat_axis=0, tiled=True)
    alignment_output = jnp.transpose(columns.reshape(32, 48, 256), (1, 0, 2))
    return alignment_output, pair_output


def solution(mesh):
    parts = Mesh(mesh.devices.reshape(2, 4, 2, 2, 2, 2), ALL)
    stack = P(SEQ, RES, None)
    in_specs = (stack, P(SEQ, RES), P(), P(RES, SEQ, None)) + (P(),) * 14
    out_specs = (stack, P(RES, SEQ, None))
    return jax.shard_map(body, mesh=parts, in_specs=in_specs, out_specs=out_specs, check_vma=False)
```

```python
import math

import jax
import jax.numpy as jnp
from jax import lax
from jax.experimental import pallas as pl
from jax.experimental.pallas import tpu as pltpu
from jax.sharding import Mesh
from jax.sharding import PartitionSpec as P

HEADS = 8
HEAD = 32
F32 = jnp.float32
BF16 = jnp.bfloat16
NEG = -1e9
STEP = 3
PICK = 2
SEQ = ("yh", "z")
RES = ("yl", "xh", "xl", "core")
ALL = SEQ + RES
TEAM = ("yl", "xh")
PLANE = SEQ + TEAM
NT = (((1,), (1,)), ((), ()))
TN = (((0,), (0,)), ((), ()))
VMEM_LIMIT = 24 * 1024 * 1024
LOG2E = math.log2(math.e)


def normalize(values):
    values = values.astype(F32)
    center = values - jnp.mean(values, axis=-1, keepdims=True)
    spread = jnp.mean(center * center, axis=-1, keepdims=True)
    return (center * lax.rsqrt(spread + 1e-5)).astype(BF16)


def project(values, weight):
    return jnp.dot(values, weight, preferred_element_type=F32)


class Attention:
    def __init__(self, query_t, key, value_t, bias_of, mask_lanes, lane, heads):
        self.query_t, self.key, self.value_t = query_t, key, value_t
        self.bias_of, self.mask_lanes, self.lane = bias_of, mask_lanes, lane
        self.heads = heads
        self.units = HEADS // heads
        self.count = query_t.shape[1]
        self.found = []

    def score(self, unit):
        first = unit * self.heads
        part = slice(first // 4 * 128, first // 4 * 128 + 128)
        own = self.query_t[part]
        row = lax.broadcasted_iota(jnp.int32, own.shape, 0)
        one = jnp.where(row == self.lane, 1.0, 0.0).astype(BF16)
        stacked = []
        for h in range(self.heads):
            mine = row // HEAD == first % 4 + h
            stacked.append(jnp.concatenate([jnp.where(mine, own, jnp.zeros_like(own)), one], axis=0))
        keys = jnp.concatenate([self.key[:, part], self.mask_lanes], axis=1)
        return project(keys, jnp.concatenate(stacked, axis=1))

    def weigh(self, unit, scores):
        weights = []
        for h in range(self.heads):
            extra = self.bias_of(unit * self.heads + h)
            for low in range(0, self.count, 128):
                tile = scores[:, h * self.count + low : h * self.count + low + 128]
                if extra is not None:
                    tile = tile + extra[:, low : low + 128]
                weights.append(jnp.exp2(tile - jnp.max(tile, axis=0, keepdims=True)).astype(BF16))
        return jnp.concatenate(weights, axis=1)

    def mix(self, unit, weights):
        size = self.heads * HEAD
        ones = jnp.ones((16, self.value_t.shape[1]), BF16)
        values = jnp.concatenate([self.value_t[unit * size : (unit + 1) * size], ones], axis=0)
        mixed = project(values, weights)
        for h in range(self.heads):
            cols = slice(h * self.count, (h + 1) * self.count)
            self.found.append(mixed[h * HEAD : (h + 1) * HEAD, cols] / mixed[size : size + 1, cols])

    def result(self):
        return jnp.concatenate(self.found, axis=0)


def run_pipelined(attentions, finish):
    units = [(a, unit) for a in attentions for unit in range(a.units)]
    ahead = units[0][0].score(0)
    for place, (attention, unit) in enumerate(units):
        scores = ahead
        if place + 1 < len(units):
            ahead = units[place + 1][0].score(units[place + 1][1])
        attention.mix(unit, attention.weigh(unit, scores))
        if unit == attention.units - 1:
            finish(attentions.index(attention), attention.result())


def mask_columns(mask_row):
    shape = (128, mask_row.shape[1])
    top = lax.broadcasted_iota(jnp.int32, shape, 0) == 0
    return jnp.where(top, jnp.broadcast_to(mask_row, shape), 0.0).astype(BF16).T


def factor_kernel(x_ref, mask_ref, source_ref, target_ref, left_ref, right_ref, lefts, rights):
    ln = normalize(x_ref[...].reshape(1536, 256))
    mask = mask_ref[...].astype(F32).T
    lefts[:, :32] = lax.dot_general(ln, source_ref[...], NT, preferred_element_type=F32)
    turned = lax.dot_general(target_ref[...], ln, NT, preferred_element_type=F32)
    for s in range(48):
        rights[s * 32 : (s + 1) * 32, :32] = turned[:, s * 32 : (s + 1) * 32]
    wide = jnp.concatenate([mask] * 4, axis=1)
    for tile in range(8):
        lanes = slice(tile * 128, (tile + 1) * 128)
        spots = [pl.ds(tile * 4 + e, 48, stride=32) for e in range(4)]
        parts = [lefts[spot, :][:, :32] for spot in spots]
        parts = [p * mask[:, tile * 4 + e : tile * 4 + e + 1] for e, p in enumerate(parts)]
        left_ref[:, lanes] = jnp.concatenate(parts, axis=1).astype(BF16)
        parts = [rights[spot, :][:, :32] for spot in spots]
        right_ref[:, lanes] = (jnp.concatenate(parts, axis=1) * wide).astype(BF16)
    tail = jnp.concatenate([mask, jnp.zeros((48, 96), F32)], axis=1).astype(BF16)
    left_ref[:, 1024:] = tail
    right_ref[:, 1024:] = tail


def pair_kernel(at_ref, *refs):
    left_pieces = refs[:4]
    mine_ref, other_ref, pair_ref, rows_ref, cols_ref, final_ref, offset_ref = refs[4:11]
    out_ref, bias_ref, column_ref, left_hold, right_hold, hold = refs[11:]
    seq_at, core = at_ref[0], at_ref[1]
    for k in range(8):
        place = k // 4 * 4 + (k + 8 - seq_at) % 4
        right_hold[core, place] = mine_ref[k]
        right_hold[1 - core, place] = other_ref[k]
    for k in range(8):
        left_hold[seq_at ^ k] = left_pieces[k % 4][k // 4]
    left_all = left_hold[...].reshape(384, 1152)
    right = [right_hold[p].reshape(384, 1152) for p in range(2)]
    left_mask = left_all[:, 1024:1056]
    picks = lax.broadcasted_iota(jnp.int32, (8, 32), 0) + seq_at * 4
    picks = (picks == lax.broadcasted_iota(jnp.int32, (8, 32), 1)).astype(BF16)
    present = lax.dot_general(picks, left_mask, NT, preferred_element_type=F32)
    column_ref[...] = (present - 1.0) * -NEG
    count = jnp.concatenate(
        [
            lax.dot_general(r[:, 1024:1056], left_mask, TN, preferred_element_type=F32)
            for r in right
        ],
        axis=0,
    )
    factor = cols_ref[...] * rows_ref[...] / (count + 0.001)
    offset = offset_ref[...]
    def outer_of(block):
        left = left_all[:, block * 1024 : (block + 1) * 1024]
        return [
            lax.dot_general(left, r[:, :1024], TN, preferred_element_type=F32).astype(BF16)
            for r in right
        ]

    for block in range(1):
        outer = outer_of(block)
        turned = []
        for i in range(32):
            for p in range(2):
                rows = outer[p][i * 32 : (i + 1) * 32]
                tiles = [rows[:, t * 128 : (t + 1) * 128] for t in range(8)]
                turned.append(jnp.concatenate(tiles, axis=0).T)
        terms = None
        for e in range(4):
            lhs = jnp.concatenate([t[e * 32 : (e + 1) * 32] for t in turned], axis=0)
            part = project(lhs, final_ref[e])
            terms = part if terms is None else terms + part
        for i in range(32):
            at = block * 32 + i
            sums = terms[i * 64 : (i + 1) * 64]
            fresh = pair_ref[at].astype(F32) + factor[:, at : at + 1] * sums
            fresh = fresh.astype(BF16)
            out_ref[at] = fresh
            bias = lax.dot_general(offset, normalize(fresh), NT, preferred_element_type=F32)
            hold[:, at : at + 1, :] = bias[:, None, :]
    for h in range(8):
        turned = hold[h].T
        quarters = [turned[q * 16 : (q + 1) * 16] for q in range(4)]
        block = jnp.concatenate(quarters, axis=1).astype(BF16)
        for reader in range(32):
            bias_ref[reader, h] = block


def ready_kernel(at_ref, *refs):
    x_ref, xc_ref, xx_ref, xxc_ref = refs[:4]
    tails = refs[4:8]
    wq_ref, wk_ref, wv_ref, wg_ref = refs[8:12]
    query_ref, key_ref, value_ref, gate_ref, mask_ref, ordered, columns = refs[12:]
    xl, core = at_ref[0], at_ref[1]

    @pl.when(pl.program_id(0) == 0)
    def _():
        columns[...] = jnp.zeros_like(columns)
        places = [(xl, core), (xl, 1 - core), (1 - xl, core), (1 - xl, 1 - core)]
        for tail_ref, (a, b) in zip(tails, places):
            for u in range(4):
                absent = ((tail_ref[u, :, :128].astype(F32) - 1.0) * -NEG).T
                columns[u, a, b, :, :16] = absent[:32]
        mask_ref[...] = columns[...].reshape(512, 128).astype(BF16)

    for t in range(STEP):
        rows = slice(t * 32, (t + 1) * 32)
        asked = normalize(x_ref[:, rows].reshape(128, 256))
        ordered[t, :, xl, core] = asked.reshape(4, 32, 256)
        ordered[t, :, xl, 1 - core] = normalize(xc_ref[:, rows])
        ordered[t, :, 1 - xl, core] = normalize(xx_ref[:, rows])
        ordered[t, :, 1 - xl, 1 - core] = normalize(xxc_ref[:, rows])
        keys = ordered[t].reshape(512, 256)
        query_ref[t] = (project(asked, wq_ref[...]) * (HEAD**-0.5 * LOG2E)).T.astype(BF16)
        key_ref[t] = project(keys, wk_ref[...]).astype(BF16)
        value_ref[t] = project(keys, wv_ref[...]).astype(BF16).T
        gate_ref[t] = jax.nn.sigmoid(project(asked, wg_ref[...])).T


def row_kernel(
    x_ref, query_ref, key_ref, value_ref, gate_ref, mask_ref, bias_ref, wo_ref, out_ref, held
):
    @pl.when(pl.program_id(0) == 0)
    def _():
        for a in range(8):
            for j in range(4):
                low = a * 64 + j * 16
                parts = [bias_ref[a, q, :, :, j * 32 : (j + 1) * 32] for q in range(4)]
                part = jnp.concatenate(parts, axis=2).astype(F32)
                held[:, low : low + 16] = part * LOG2E

    def finish(t, found):
        gated = (gate_ref[t] * found).astype(BF16)
        update = lax.dot_general(gated, wo_ref[...], TN, preferred_element_type=F32).astype(BF16)
        raw = x_ref[:, t * 32 : (t + 1) * 32].reshape(128, 256)
        out_ref[t] = (raw.astype(F32) + update.astype(F32)).astype(BF16)

    attentions = [
        Attention(
            query_ref[t],
            key_ref[t],
            value_ref[t],
            lambda h: held[h],
            mask_ref[...],
            pl.program_id(0) * STEP + t,
            4,
        )
        for t in range(STEP)
    ]
    run_pipelined(attentions, finish)


def column_kernel(x_ref, mask_ref, wq_ref, wk_ref, wv_ref, wg_ref, wo_ref, out_ref):
    keys = normalize(x_ref[...].reshape(PICK * 384, 256))
    key = project(keys, wk_ref[...]).astype(BF16)
    weights = jnp.concatenate([wq_ref[...], wv_ref[...], wg_ref[...]], axis=1)
    turned = lax.dot_general(weights, keys.T, TN, preferred_element_type=F32)
    query_t = (turned[:256] * (HEAD**-0.5 * LOG2E)).astype(BF16)
    value_t = turned[256:512].astype(BF16)
    gate = jax.nn.sigmoid(turned[512:])
    gates, attentions = [], []
    for r in range(PICK):
        rows = slice(r * 384, (r + 1) * 384)
        gates.append(gate[:, rows])
        mask = mask_columns(mask_ref[pl.ds(pl.program_id(0) * PICK + r, 1), :])
        attentions.append(
            Attention(query_t[:, rows], key[rows], value_t[:, rows], lambda h: None, mask, 0, 2)
        )

    def finish(r, found):
        gated = (gates[r] * found).astype(BF16)
        update = lax.dot_general(gated, wo_ref[...], TN, preferred_element_type=F32).astype(BF16)
        out_ref[r] = (x_ref[r].astype(F32) + update.astype(F32)).astype(BF16)

    run_pipelined(attentions, finish)


def in_hbm(array):
    return pltpu.with_memory_space_constraint(array, pltpu.HBM)


def spread(block, axes, count):
    wide = jnp.broadcast_to(block[None], (count,) + block.shape)
    return lax.all_to_all(wide, axes, split_axis=0, concat_axis=0, tiled=True)


def whole(shape):
    zeros = (0,) * len(shape)
    return pl.BlockSpec(shape, lambda *_: zeros)


def body(
    homolog_stack,
    entry_exists_flags,
    genuine_amino_flags,
    couplings_tensor,
    product_source_weights,
    product_target_weights,
    product_final_weights,
    coupling_logit_offset,
    horizontal_asking_weights,
    horizontal_lookup_weights,
    horizontal_content_weights,
    horizontal_sigmoid_weights,
    horizontal_final_weights,
    vertical_asking_weights,
    vertical_lookup_weights,
    vertical_content_weights,
    vertical_sigmoid_weights,
    vertical_final_weights,
):
    seq_at = lax.axis_index(SEQ)
    res_at = lax.axis_index(RES)
    xl_at = lax.axis_index("xl")
    core_at = lax.axis_index("core")
    mask = entry_exists_flags.astype(BF16)

    tail = jnp.pad(mask.reshape(4, 12, 32), ((0, 0), (0, 4), (0, 224)))
    packed = jnp.concatenate([homolog_stack.reshape(4, 384, 256), tail], axis=1)
    team_at = lax.axis_index(TEAM)
    parts = []
    for k in range(4):
        part = lax.dynamic_index_in_dim(packed, team_at ^ k, 0, False)
        parts.append(lax.ppermute(part, TEAM, [(t, t ^ k) for t in range(4)]) if k else part)
    packed = jnp.stack(parts).reshape(2, 2, 400, 256)
    packed = jnp.where(lax.axis_index("yl") == 1, packed[::-1], packed)
    packed = jnp.where(lax.axis_index("xh") == 1, packed[:, ::-1], packed)
    packed = packed.reshape(4, 400, 256)

    left, right = pl.pallas_call(
        factor_kernel,
        out_shape=[jax.ShapeDtypeStruct((48, 1152), BF16)] * 2,
        scratch_shapes=[pltpu.VMEM((1536, 128), F32)] * 2,
        compiler_params=pltpu.CompilerParams(vmem_limit_bytes=VMEM_LIMIT),
        name="factors",
    )(
        in_hbm(homolog_stack),
        in_hbm(entry_exists_flags.T),
        in_hbm(product_source_weights.T),
        in_hbm(product_target_weights.T),
    )
    swap = [
        ((a * 8 + b) * 2 + p, (b * 8 + a // 4 * 4 + (a + b) % 4) * 2 + p)
        for a in range(8)
        for b in range(8)
        for p in range(2)
    ]
    pairs = [(0, 1), (1, 0)]
    right = lax.ppermute(right, ALL, swap)
    left_yh = lax.ppermute(left, "yh", pairs)
    right, left_yh, packed = lax.optimization_barrier((right, left_yh, packed))
    mine = spread(right, ("yl", "xh", "xl"), 8)
    left = jnp.stack([left, left_yh])
    lefts = [left] + [
        lax.ppermute(left, "z", [(z, z ^ k) for z in range(4)]) for k in range(1, 4)
    ]
    final = product_final_weights.reshape(32, 8, 4, 128)
    final = jnp.transpose(final, (2, 1, 0, 3)).reshape(4, 256, 128)
    mine, final, *lefts = lax.optimization_barrier((mine, final, *lefts))
    other = lax.ppermute(mine, "core", pairs)
    packed_x = lax.ppermute(packed, "xl", pairs)
    packed_c = lax.ppermute(packed, "core", pairs)

    flags = genuine_amino_flags.astype(F32)
    row_flags = lax.dynamic_slice_in_dim(flags, res_at * 32, 32).reshape(1, 32)
    col_flags = lax.dynamic_slice_in_dim(flags, seq_at * 64, 64).reshape(64, 1)
    square = whole((256, 256))
    smem = pl.BlockSpec(memory_space=pltpu.SMEM)
    vmem = pl.BlockSpec(memory_space=pltpu.VMEM)
    pair_output, bias, col_mask = pl.pallas_call(
        pair_kernel,
        out_shape=(
            jax.ShapeDtypeStruct((32, 64, 128), BF16),
            jax.ShapeDtypeStruct((32, 8, 16, 128), BF16),
            jax.ShapeDtypeStruct((8, 384), F32),
        ),
        in_specs=[smem] + [vmem] * 11,
        scratch_shapes=[
            pltpu.VMEM((8, 48, 1152), BF16),
            pltpu.VMEM((2, 8, 48, 1152), BF16),
            pltpu.VMEM((8, 32, 64), F32),
        ],
        compiler_params=pltpu.CompilerParams(vmem_limit_bytes=VMEM_LIMIT),
        cost_estimate=pl.CostEstimate(
            flops=1000, transcendentals=0, bytes_accessed=1000
        ),
        name="pair",
    )(
        jnp.stack([seq_at, core_at]).astype(jnp.int32),
        *lefts,
        mine,
        other,
        couplings_tensor,
        row_flags,
        col_flags,
        final,
        coupling_logit_offset.T,
    )

    packed, packed_c, packed_x, _ = lax.optimization_barrier((packed, packed_c, packed_x, bias))
    packed_xc = lax.ppermute(packed_x, "core", pairs)
    pieces = [in_hbm(p) for p in (packed, packed_c, packed_x)] + [packed_xc]
    by_row = [(12, 256, 128), (12, 512, 256), (12, 256, 512), (12, 256, 128)]
    specs = [pl.BlockSpec((STEP,) + shape[1:], lambda t: (t, 0, 0)) for shape in by_row]
    rows_in = pl.pallas_call(
        ready_kernel,
        out_shape=[
            pltpu.HBM(shape, kind)
            for shape, kind in zip(by_row, (BF16, BF16, BF16, F32))
        ]
        + [pltpu.HBM((512, 128), BF16)],
        grid=(12 // STEP,),
        in_specs=[smem] + [pl.BlockSpec((4, STEP * 32, 256), lambda t: (0, t, 0))] * 4
        + [pl.BlockSpec((4, 16, 256), lambda t: (0, 24, 0))] * 4
        + [square] * 4,
        out_specs=specs + [whole((512, 128))],
        scratch_shapes=[
            pltpu.VMEM((STEP, 4, 2, 2, 32, 256), BF16),
            pltpu.VMEM((4, 2, 2, 32, 128), F32),
        ],
        compiler_params=pltpu.CompilerParams(vmem_limit_bytes=VMEM_LIMIT),
        cost_estimate=pl.CostEstimate(flops=1000, transcendentals=0, bytes_accessed=1000),
        name="ready",
    )(
        jnp.stack([xl_at, core_at]).astype(jnp.int32),
        *pieces,
        *pieces,
        in_hbm(horizontal_asking_weights),
        in_hbm(horizontal_lookup_weights),
        in_hbm(horizontal_content_weights),
        in_hbm(horizontal_sigmoid_weights),
    )
    bias = lax.all_to_all(bias, PLANE, split_axis=0, concat_axis=0, tiled=True)
    bias = bias.reshape(8, 4, 8, 16, 128)

    rows_in = [in_hbm(a) for a in rows_in]
    middle = pl.pallas_call(
        row_kernel,
        out_shape=jax.ShapeDtypeStruct((12, 128, 256), BF16),
        grid=(12 // STEP,),
        in_specs=[pl.BlockSpec((4, STEP * 32, 256), lambda t: (0, t, 0))]
        + specs
        + [whole((512, 128)), whole((8, 4, 8, 16, 128)), square],
        out_specs=pl.BlockSpec((STEP, 128, 256), lambda t: (t, 0, 0)),
        scratch_shapes=[pltpu.VMEM((8, 512, 128), F32)],
        compiler_params=pltpu.CompilerParams(vmem_limit_bytes=VMEM_LIMIT),
        cost_estimate=pl.CostEstimate(
            flops=8_000_000_000, transcendentals=6_300_000, bytes_accessed=12_000_000
        ),
        name="rows",
    )(pieces[0], *rows_in, bias, horizontal_final_weights)

    middle = jnp.transpose(middle.reshape(12, 4, 8, 4, 256), (2, 1, 0, 3, 4))
    middle = lax.all_to_all(
        middle.reshape(32, 12, 4, 256), PLANE, split_axis=0, concat_axis=0, tiled=True
    )
    middle = jnp.transpose(middle.reshape(384, 4, 256), (1, 0, 2))
    columns = pl.pallas_call(
        column_kernel,
        out_shape=jax.ShapeDtypeStruct((4, 384, 256), BF16),
        grid=(4 // PICK,),
        in_specs=[
            pl.BlockSpec((PICK, 384, 256), lambda r: (r, 0, 0)),
            whole((8, 384)),
            square,
            square,
            square,
            square,
            square,
        ],
        out_specs=pl.BlockSpec((PICK, 384, 256), lambda r: (r, 0, 0)),
        compiler_params=pltpu.CompilerParams(vmem_limit_bytes=VMEM_LIMIT),
        cost_estimate=pl.CostEstimate(
            flops=8_000_000_000, transcendentals=4_700_000, bytes_accessed=2_000_000
        ),
        name="columns",
    )(
        middle,
        col_mask,
        vertical_asking_weights,
        vertical_lookup_weights,
        vertical_content_weights,
        vertical_sigmoid_weights,
        vertical_final_weights,
    )
    columns = jnp.transpose(columns.reshape(4, 8, 48, 256), (1, 0, 2, 3))
    columns = lax.all_to_all(columns, SEQ, split_axis=0, concat_axis=0, tiled=True)
    alignment_output = jnp.transpose(columns.reshape(32, 48, 256), (1, 0, 2))
    return alignment_output, pair_output


def solution(mesh):
    parts = Mesh(mesh.devices.reshape(2, 4, 2, 2, 2, 2), ALL)
    stack = P(SEQ, RES, None)
    in_specs = (stack, P(SEQ, RES), P(), P(RES, SEQ, None)) + (P(),) * 14
    out_specs = (stack, P(RES, SEQ, None))
    return jax.shard_map(body, mesh=parts, in_specs=in_specs, out_specs=out_specs, check_vma=False)
```

```python
import math

import jax
import jax.numpy as jnp
from jax import lax
from jax.experimental import pallas as pl
from jax.experimental.pallas import tpu as pltpu
from jax.sharding import Mesh
from jax.sharding import PartitionSpec as P

HEADS = 8
HEAD = 32
F32 = jnp.float32
BF16 = jnp.bfloat16
NEG = -1e9
STEP = 3
TURN = 4
PICK = 2
SEQ = ("yh", "z")
RES = ("yl", "xh", "xl", "core")
ALL = SEQ + RES
TEAM = ("yl", "xh")
PLANE = SEQ + TEAM
NT = (((1,), (1,)), ((), ()))
TN = (((0,), (0,)), ((), ()))
VMEM_LIMIT = 24 * 1024 * 1024
LOG2E = math.log2(math.e)


def normalize(values):
    values = values.astype(F32)
    center = values - jnp.mean(values, axis=-1, keepdims=True)
    spread = jnp.mean(center * center, axis=-1, keepdims=True)
    return (center * lax.rsqrt(spread + 1e-5)).astype(BF16)


def project(values, weight):
    return jnp.dot(values, weight, preferred_element_type=F32)


class Attention:
    def __init__(self, query_t, key, value_t, bias_of, mask_lanes, lane, heads):
        self.query_t, self.key, self.value_t = query_t, key, value_t
        self.bias_of, self.mask_lanes, self.lane = bias_of, mask_lanes, lane
        self.heads = heads
        self.units = HEADS // heads
        self.count = query_t.shape[1]
        self.found = []

    def score(self, unit):
        first = unit * self.heads
        part = slice(first // 4 * 128, first // 4 * 128 + 128)
        own = self.query_t[part]
        row = lax.broadcasted_iota(jnp.int32, own.shape, 0)
        one = jnp.where(row == self.lane, 1.0, 0.0).astype(BF16)
        stacked = []
        for h in range(self.heads):
            mine = row // HEAD == first % 4 + h
            stacked.append(jnp.concatenate([jnp.where(mine, own, jnp.zeros_like(own)), one], axis=0))
        keys = jnp.concatenate([self.key[:, part], self.mask_lanes], axis=1)
        return project(keys, jnp.concatenate(stacked, axis=1))

    def weigh(self, unit, scores):
        weights = []
        for h in range(self.heads):
            extra = self.bias_of(unit * self.heads + h)
            for low in range(0, self.count, 128):
                tile = scores[:, h * self.count + low : h * self.count + low + 128]
                if extra is not None:
                    tile = tile + extra[:, low : low + 128]
                weights.append(jnp.exp2(tile - jnp.max(tile, axis=0, keepdims=True)).astype(BF16))
        return jnp.concatenate(weights, axis=1)

    def mix(self, unit, weights):
        size = self.heads * HEAD
        ones = jnp.ones((16, self.value_t.shape[1]), BF16)
        values = jnp.concatenate([self.value_t[unit * size : (unit + 1) * size], ones], axis=0)
        mixed = project(values, weights)
        for h in range(self.heads):
            cols = slice(h * self.count, (h + 1) * self.count)
            self.found.append(mixed[h * HEAD : (h + 1) * HEAD, cols] / mixed[size : size + 1, cols])

    def result(self):
        return jnp.concatenate(self.found, axis=0)


def run_pipelined(attentions, finish):
    units = [(a, unit) for a in attentions for unit in range(a.units)]
    ahead = units[0][0].score(0)
    for place, (attention, unit) in enumerate(units):
        scores = ahead
        if place + 1 < len(units):
            ahead = units[place + 1][0].score(units[place + 1][1])
        attention.mix(unit, attention.weigh(unit, scores))
        if unit == attention.units - 1:
            finish(attentions.index(attention), attention.result())


def mask_columns(mask_row):
    shape = (128, mask_row.shape[1])
    top = lax.broadcasted_iota(jnp.int32, shape, 0) == 0
    return jnp.where(top, jnp.broadcast_to(mask_row, shape), 0.0).astype(BF16).T


def factor_kernel(x_ref, mask_ref, source_ref, target_ref, left_ref, right_ref, lefts, rights):
    ln = normalize(x_ref[...].reshape(1536, 256))
    mask = mask_ref[...].astype(F32).T
    lefts[:, :32] = lax.dot_general(ln, source_ref[...], NT, preferred_element_type=F32)
    turned = lax.dot_general(target_ref[...], ln, NT, preferred_element_type=F32)
    for s in range(48):
        rights[s * 32 : (s + 1) * 32, :32] = turned[:, s * 32 : (s + 1) * 32]
    wide = jnp.concatenate([mask] * 4, axis=1)
    for tile in range(8):
        lanes = slice(tile * 128, (tile + 1) * 128)
        spots = [pl.ds(tile * 4 + e, 48, stride=32) for e in range(4)]
        parts = [lefts[spot, :][:, :32] for spot in spots]
        parts = [p * mask[:, tile * 4 + e : tile * 4 + e + 1] for e, p in enumerate(parts)]
        left_ref[:, lanes] = jnp.concatenate(parts, axis=1).astype(BF16)
        parts = [rights[spot, :][:, :32] for spot in spots]
        right_ref[:, lanes] = (jnp.concatenate(parts, axis=1) * wide).astype(BF16)
    tail = jnp.concatenate([mask, jnp.zeros((48, 96), F32)], axis=1).astype(BF16)
    left_ref[:, 1024:] = tail
    right_ref[:, 1024:] = tail


def pair_kernel(at_ref, *refs):
    left_pieces = refs[:4]
    mine_ref, other_ref, pair_ref, rows_ref, cols_ref, final_ref, offset_ref = refs[4:11]
    out_ref, bias_ref, column_ref, left_hold, right_hold, hold = refs[11:]
    seq_at, core = at_ref[0], at_ref[1]
    for k in range(8):
        place = k // 4 * 4 + (k + 8 - seq_at) % 4
        right_hold[core, place] = mine_ref[k]
        right_hold[1 - core, place] = other_ref[k]
    for k in range(8):
        left_hold[seq_at ^ k] = left_pieces[k % 4][k // 4]
    left_all = left_hold[...].reshape(384, 1152)
    right = [right_hold[p].reshape(384, 1152) for p in range(2)]
    left_mask = left_all[:, 1024:1056]
    picks = lax.broadcasted_iota(jnp.int32, (8, 32), 0) + seq_at * 4
    picks = (picks == lax.broadcasted_iota(jnp.int32, (8, 32), 1)).astype(BF16)
    present = lax.dot_general(picks, left_mask, NT, preferred_element_type=F32)
    column_ref[...] = (present - 1.0) * -NEG
    count = jnp.concatenate(
        [
            lax.dot_general(r[:, 1024:1056], left_mask, TN, preferred_element_type=F32)
            for r in right
        ],
        axis=0,
    )
    factor = cols_ref[...] * rows_ref[...] / (count + 0.001)
    offset = offset_ref[...]
    def outer_of(block):
        left = left_all[:, block * 1024 : (block + 1) * 1024]
        return [
            lax.dot_general(left, r[:, :1024], TN, preferred_element_type=F32).astype(BF16)
            for r in right
        ]

    for block in range(1):
        outer = outer_of(block)
        turned = []
        for i in range(32):
            for p in range(2):
                rows = outer[p][i * 32 : (i + 1) * 32]
                tiles = [rows[:, t * 128 : (t + 1) * 128] for t in range(8)]
                turned.append(jnp.concatenate(tiles, axis=0).T)
        terms = None
        for e in range(4):
            lhs = jnp.concatenate([t[e * 32 : (e + 1) * 32] for t in turned], axis=0)
            part = project(lhs, final_ref[e])
            terms = part if terms is None else terms + part
        for i in range(32):
            at = block * 32 + i
            sums = terms[i * 64 : (i + 1) * 64]
            fresh = pair_ref[at].astype(F32) + factor[:, at : at + 1] * sums
            fresh = fresh.astype(BF16)
            out_ref[at] = fresh
            bias = lax.dot_general(offset, normalize(fresh), NT, preferred_element_type=F32)
            hold[:, at : at + 1, :] = bias[:, None, :]
    for h in range(8):
        turned = hold[h].T
        quarters = [turned[q * 16 : (q + 1) * 16] for q in range(4)]
        block = jnp.concatenate(quarters, axis=1).astype(BF16)
        for reader in range(32):
            bias_ref[reader, h] = block


def ready_kernel(at_ref, *refs):
    x_ref, xc_ref, xx_ref, xxc_ref = refs[:4]
    tails = refs[4:8]
    wq_ref, wk_ref, wv_ref, wg_ref = refs[8:12]
    query_ref, key_ref, value_ref, gate_ref, mask_ref, ordered, columns = refs[12:]
    xl, core = at_ref[0], at_ref[1]

    @pl.when(pl.program_id(0) == 0)
    def _():
        places = [(xl, core), (xl, 1 - core), (1 - xl, core), (1 - xl, 1 - core)]
        for tail_ref, (a, b) in zip(tails, places):
            columns[:, a, b] = (tail_ref[:, :, :128].astype(F32) - 1.0) * -NEG
        mask_ref[...] = columns[...].reshape(512, 128).astype(BF16)

    for t in range(STEP):
        rows = slice(t * 32, (t + 1) * 32)
        asked = normalize(x_ref[:, rows].reshape(128, 256))
        ordered[t, :, xl, core] = asked.reshape(4, 32, 256)
        ordered[t, :, xl, 1 - core] = normalize(xc_ref[:, rows])
        ordered[t, :, 1 - xl, core] = normalize(xx_ref[:, rows])
        ordered[t, :, 1 - xl, 1 - core] = normalize(xxc_ref[:, rows])
        keys = ordered[t].reshape(512, 256)
        query_ref[t] = (project(asked, wq_ref[...]) * (HEAD**-0.5 * LOG2E)).T.astype(BF16)
        key_ref[t] = project(keys, wk_ref[...]).astype(BF16)
        value_ref[t] = project(keys, wv_ref[...]).astype(BF16).T
        gate_ref[t] = jax.nn.sigmoid(project(asked, wg_ref[...])).T


def row_kernel(
    at_ref, x_ref, query_ref, key_ref, value_ref, gate_ref, mask_ref, bias_ref, wo_ref, out_ref, held
):
    @pl.when(pl.program_id(0) == 0)
    def _():
        for a in range(8):
            for j in range(4):
                low = a * 64 + j * 16
                parts = [bias_ref[a, q, :, :, j * 32 : (j + 1) * 32] for q in range(4)]
                part = jnp.concatenate(parts, axis=2).astype(F32)
                held[:, low : low + 16] = part * LOG2E

    def finish(t, found):
        gated = (gate_ref[t] * found).astype(BF16)
        update = lax.dot_general(gated, wo_ref[...], TN, preferred_element_type=F32).astype(BF16)
        raw = x_ref[:, t * 32 : (t + 1) * 32].reshape(128, 256)
        out_ref[t] = (raw.astype(F32) + update.astype(F32)).astype(BF16)

    attentions = [
        Attention(
            query_ref[t],
            key_ref[t],
            value_ref[t],
            lambda h: held[h],
            mask_ref[...],
            at_ref[0] * 12 + pl.program_id(0) * TURN + t,
            4,
        )
        for t in range(TURN)
    ]
    run_pipelined(attentions, finish)


def column_kernel(x_ref, mask_ref, wq_ref, wk_ref, wv_ref, wg_ref, wo_ref, out_ref):
    keys = normalize(x_ref[...].reshape(PICK * 384, 256))
    key = project(keys, wk_ref[...]).astype(BF16)
    weights = jnp.concatenate([wq_ref[...], wv_ref[...], wg_ref[...]], axis=1)
    turned = lax.dot_general(weights, keys.T, TN, preferred_element_type=F32)
    query_t = (turned[:256] * (HEAD**-0.5 * LOG2E)).astype(BF16)
    value_t = turned[256:512].astype(BF16)
    gate = jax.nn.sigmoid(turned[512:])
    gates, attentions = [], []
    for r in range(PICK):
        rows = slice(r * 384, (r + 1) * 384)
        gates.append(gate[:, rows])
        mask = mask_columns(mask_ref[pl.ds(pl.program_id(0) * PICK + r, 1), :])
        attentions.append(
            Attention(query_t[:, rows], key[rows], value_t[:, rows], lambda h: None, mask, 0, 2)
        )

    def finish(r, found):
        gated = (gates[r] * found).astype(BF16)
        update = lax.dot_general(gated, wo_ref[...], TN, preferred_element_type=F32).astype(BF16)
        out_ref[r] = (x_ref[r].astype(F32) + update.astype(F32)).astype(BF16)

    run_pipelined(attentions, finish)


def in_hbm(array):
    return pltpu.with_memory_space_constraint(array, pltpu.HBM)


def spread(block, axes, count):
    wide = jnp.broadcast_to(block[None], (count,) + block.shape)
    return lax.all_to_all(wide, axes, split_axis=0, concat_axis=0, tiled=True)


def whole(shape):
    zeros = (0,) * len(shape)
    return pl.BlockSpec(shape, lambda *_: zeros)


def body(
    homolog_stack,
    entry_exists_flags,
    genuine_amino_flags,
    couplings_tensor,
    product_source_weights,
    product_target_weights,
    product_final_weights,
    coupling_logit_offset,
    horizontal_asking_weights,
    horizontal_lookup_weights,
    horizontal_content_weights,
    horizontal_sigmoid_weights,
    horizontal_final_weights,
    vertical_asking_weights,
    vertical_lookup_weights,
    vertical_content_weights,
    vertical_sigmoid_weights,
    vertical_final_weights,
):
    seq_at = lax.axis_index(SEQ)
    res_at = lax.axis_index(RES)
    xl_at = lax.axis_index("xl")
    core_at = lax.axis_index("core")

    tail = jnp.pad(entry_exists_flags.T.astype(BF16), ((0, 0), (0, 208)))
    tail = jnp.broadcast_to(tail[None], (4, 32, 256))
    packed = jnp.concatenate([homolog_stack.reshape(4, 384, 256), tail], axis=1)
    team_at = lax.axis_index(TEAM)
    parts = []
    for k in range(4):
        part = lax.dynamic_index_in_dim(packed, team_at ^ k, 0, False)
        parts.append(lax.ppermute(part, TEAM, [(t, t ^ k) for t in range(4)]) if k else part)
    packed = jnp.stack(parts).reshape(2, 2, 416, 256)
    packed = jnp.where(lax.axis_index("yl") == 1, packed[::-1], packed)
    packed = jnp.where(lax.axis_index("xh") == 1, packed[:, ::-1], packed)
    packed = packed.reshape(4, 416, 256)

    left, right = pl.pallas_call(
        factor_kernel,
        out_shape=[jax.ShapeDtypeStruct((48, 1152), BF16)] * 2,
        scratch_shapes=[pltpu.VMEM((1536, 128), F32)] * 2,
        compiler_params=pltpu.CompilerParams(vmem_limit_bytes=VMEM_LIMIT),
        name="factors",
    )(
        in_hbm(homolog_stack),
        in_hbm(entry_exists_flags.T),
        in_hbm(product_source_weights.T),
        in_hbm(product_target_weights.T),
    )
    swap = [
        ((a * 8 + b) * 2 + p, (b * 8 + a // 4 * 4 + (a + b) % 4) * 2 + p)
        for a in range(8)
        for b in range(8)
        for p in range(2)
    ]
    pairs = [(0, 1), (1, 0)]
    right = lax.ppermute(right, ALL, swap)
    left_yh = lax.ppermute(left, "yh", pairs)
    right, left_yh, packed = lax.optimization_barrier((right, left_yh, packed))
    mine = spread(right, ("yl", "xh", "xl"), 8)
    left = jnp.stack([left, left_yh])
    lefts = [left] + [
        lax.ppermute(left, "z", [(z, z ^ k) for z in range(4)]) for k in range(1, 4)
    ]
    final = product_final_weights.reshape(32, 8, 4, 128)
    final = jnp.transpose(final, (2, 1, 0, 3)).reshape(4, 256, 128)
    mine, final, *lefts = lax.optimization_barrier((mine, final, *lefts))
    other = lax.ppermute(mine, "core", pairs)
    packed_x = lax.ppermute(packed, "xl", pairs)
    packed_c = lax.ppermute(packed, "core", pairs)

    flags = genuine_amino_flags.astype(F32)
    row_flags = lax.dynamic_slice_in_dim(flags, res_at * 32, 32).reshape(1, 32)
    col_flags = lax.dynamic_slice_in_dim(flags, seq_at * 64, 64).reshape(64, 1)
    square = whole((256, 256))
    smem = pl.BlockSpec(memory_space=pltpu.SMEM)
    vmem = pl.BlockSpec(memory_space=pltpu.VMEM)
    pair_output, bias, col_mask = pl.pallas_call(
        pair_kernel,
        out_shape=(
            jax.ShapeDtypeStruct((32, 64, 128), BF16),
            jax.ShapeDtypeStruct((32, 8, 16, 128), BF16),
            jax.ShapeDtypeStruct((8, 384), F32),
        ),
        in_specs=[smem] + [vmem] * 11,
        scratch_shapes=[
            pltpu.VMEM((8, 48, 1152), BF16),
            pltpu.VMEM((2, 8, 48, 1152), BF16),
            pltpu.VMEM((8, 32, 64), F32),
        ],
        compiler_params=pltpu.CompilerParams(vmem_limit_bytes=VMEM_LIMIT),
        cost_estimate=pl.CostEstimate(
            flops=1000, transcendentals=0, bytes_accessed=1000
        ),
        name="pair",
    )(
        jnp.stack([seq_at, core_at]).astype(jnp.int32),
        *lefts,
        mine,
        other,
        couplings_tensor,
        row_flags,
        col_flags,
        final,
        coupling_logit_offset.T,
    )

    packed, packed_c, packed_x, _ = lax.optimization_barrier((packed, packed_c, packed_x, bias))
    packed_xc = lax.ppermute(packed_x, "core", pairs)
    pieces = [in_hbm(p) for p in (packed, packed_c, packed_x)] + [packed_xc]
    by_row = [(12, 256, 128), (12, 512, 256), (12, 256, 512), (12, 256, 128)]
    specs = [pl.BlockSpec((STEP,) + shape[1:], lambda t: (t, 0, 0)) for shape in by_row]
    rows_in = pl.pallas_call(
        ready_kernel,
        out_shape=[
            pltpu.HBM(shape, kind)
            for shape, kind in zip(by_row, (BF16, BF16, BF16, F32))
        ]
        + [pltpu.HBM((512, 128), BF16)],
        grid=(12 // STEP,),
        in_specs=[smem] + [pl.BlockSpec((4, STEP * 32, 256), lambda t: (0, t, 0))] * 4
        + [pl.BlockSpec((4, 32, 256), lambda t: (0, 12, 0))] * 4
        + [square] * 4,
        out_specs=specs + [whole((512, 128))],
        scratch_shapes=[
            pltpu.VMEM((STEP, 4, 2, 2, 32, 256), BF16),
            pltpu.VMEM((4, 2, 2, 32, 128), F32),
        ],
        compiler_params=pltpu.CompilerParams(vmem_limit_bytes=VMEM_LIMIT),
        cost_estimate=pl.CostEstimate(flops=1000, transcendentals=0, bytes_accessed=1000),
        name="ready",
    )(
        jnp.stack([xl_at, core_at]).astype(jnp.int32),
        *pieces,
        *pieces,
        in_hbm(horizontal_asking_weights),
        in_hbm(horizontal_lookup_weights),
        in_hbm(horizontal_content_weights),
        in_hbm(horizontal_sigmoid_weights),
    )
    bias = lax.all_to_all(bias, PLANE, split_axis=0, concat_axis=0, tiled=True)
    bias = bias.reshape(8, 4, 8, 16, 128)

    rows_in = [in_hbm(a) for a in rows_in]
    middle = pl.pallas_call(
        row_kernel,
        out_shape=jax.ShapeDtypeStruct((12, 128, 256), BF16),
        grid=(12 // TURN,),
        in_specs=[smem, pl.BlockSpec((4, TURN * 32, 256), lambda t: (0, t, 0))]
        + [pl.BlockSpec((TURN,) + shape[1:], lambda t: (t, 0, 0)) for shape in by_row]
        + [whole((512, 128)), whole((8, 4, 8, 16, 128)), square],
        out_specs=pl.BlockSpec((TURN, 128, 256), lambda t: (t, 0, 0)),
        scratch_shapes=[pltpu.VMEM((8, 512, 128), F32)],
        compiler_params=pltpu.CompilerParams(vmem_limit_bytes=VMEM_LIMIT),
        cost_estimate=pl.CostEstimate(
            flops=8_000_000_000, transcendentals=6_300_000, bytes_accessed=12_000_000
        ),
        name="rows",
    )(team_at.astype(jnp.int32).reshape(1), pieces[0], *rows_in, bias, horizontal_final_weights)

    middle = jnp.transpose(middle.reshape(12, 4, 8, 4, 256), (2, 1, 0, 3, 4))
    middle = lax.all_to_all(
        middle.reshape(32, 12, 4, 256), PLANE, split_axis=0, concat_axis=0, tiled=True
    )
    middle = jnp.transpose(middle.reshape(384, 4, 256), (1, 0, 2))
    columns = pl.pallas_call(
        column_kernel,
        out_shape=jax.ShapeDtypeStruct((4, 384, 256), BF16),
        grid=(4 // PICK,),
        in_specs=[
            pl.BlockSpec((PICK, 384, 256), lambda r: (r, 0, 0)),
            whole((8, 384)),
            square,
            square,
            square,
            square,
            square,
        ],
        out_specs=pl.BlockSpec((PICK, 384, 256), lambda r: (r, 0, 0)),
        compiler_params=pltpu.CompilerParams(vmem_limit_bytes=VMEM_LIMIT),
        cost_estimate=pl.CostEstimate(
            flops=8_000_000_000, transcendentals=4_700_000, bytes_accessed=2_000_000
        ),
        name="columns",
    )(
        middle,
        col_mask,
        vertical_asking_weights,
        vertical_lookup_weights,
        vertical_content_weights,
        vertical_sigmoid_weights,
        vertical_final_weights,
    )
    columns = jnp.transpose(columns.reshape(4, 8, 48, 256), (1, 0, 2, 3))
    columns = lax.all_to_all(columns, SEQ, split_axis=0, concat_axis=0, tiled=True)
    alignment_output = jnp.transpose(columns.reshape(32, 48, 256), (1, 0, 2))
    return alignment_output, pair_output


def solution(mesh):
    parts = Mesh(mesh.devices.reshape(2, 4, 2, 2, 2, 2), ALL)
    stack = P(SEQ, RES, None)
    in_specs = (stack, P(SEQ, RES), P(), P(RES, SEQ, None)) + (P(),) * 14
    out_specs = (stack, P(RES, SEQ, None))
    return jax.shard_map(body, mesh=parts, in_specs=in_specs, out_specs=out_specs, check_vma=False)
```

```python
import math

import jax
import jax.numpy as jnp
from jax import lax
from jax.experimental import pallas as pl
from jax.experimental.pallas import tpu as pltpu
from jax.sharding import Mesh
from jax.sharding import PartitionSpec as P

HEADS = 8
HEAD = 32
F32 = jnp.float32
BF16 = jnp.bfloat16
NEG = -1e9
STEP = 3
TURN = 6
PICK = 4
SEQ = ("yh", "z")
RES = ("yl", "xh", "xl", "core")
ALL = SEQ + RES
TEAM = ("yl", "xh")
PLANE = SEQ + TEAM
NT = (((1,), (1,)), ((), ()))
TN = (((0,), (0,)), ((), ()))
VMEM_LIMIT = 28 * 1024 * 1024
LOG2E = math.log2(math.e)


def normalize(values):
    values = values.astype(F32)
    center = values - jnp.mean(values, axis=-1, keepdims=True)
    spread = jnp.mean(center * center, axis=-1, keepdims=True)
    return (center * lax.rsqrt(spread + 1e-5)).astype(BF16)


def project(values, weight):
    return jnp.dot(values, weight, preferred_element_type=F32)


class Attention:
    def __init__(self, query_t, key, value_t, bias_of, mask_lanes, lane, heads):
        self.query_t, self.key, self.value_t = query_t, key, value_t
        self.bias_of, self.mask_lanes, self.lane = bias_of, mask_lanes, lane
        self.heads = heads
        self.units = HEADS // heads
        self.count = query_t.shape[1]
        self.found = []

    def score(self, unit):
        first = unit * self.heads
        part = slice(first // 4 * 128, first // 4 * 128 + 128)
        own = self.query_t[part]
        row = lax.broadcasted_iota(jnp.int32, own.shape, 0)
        one = jnp.where(row == self.lane, 1.0, 0.0).astype(BF16)
        stacked = []
        for h in range(self.heads):
            mine = row // HEAD == first % 4 + h
            stacked.append(jnp.concatenate([jnp.where(mine, own, jnp.zeros_like(own)), one], axis=0))
        keys = jnp.concatenate([self.key[:, part], self.mask_lanes], axis=1)
        return project(keys, jnp.concatenate(stacked, axis=1))

    def weigh(self, unit, scores):
        weights = []
        for h in range(self.heads):
            extra = self.bias_of(unit * self.heads + h)
            for low in range(0, self.count, 128):
                tile = scores[:, h * self.count + low : h * self.count + low + 128]
                if extra is not None:
                    tile = tile + extra[:, low : low + 128]
                weights.append(jnp.exp2(tile - jnp.max(tile, axis=0, keepdims=True)).astype(BF16))
        return jnp.concatenate(weights, axis=1)

    def mix(self, unit, weights):
        size = self.heads * HEAD
        ones = jnp.ones((16, self.value_t.shape[1]), BF16)
        values = jnp.concatenate([self.value_t[unit * size : (unit + 1) * size], ones], axis=0)
        mixed = project(values, weights)
        for h in range(self.heads):
            cols = slice(h * self.count, (h + 1) * self.count)
            self.found.append(mixed[h * HEAD : (h + 1) * HEAD, cols] / mixed[size : size + 1, cols])

    def result(self):
        return jnp.concatenate(self.found, axis=0)


def run_pipelined(attentions, finish):
    units = [(a, unit) for a in attentions for unit in range(a.units)]
    ahead = units[0][0].score(0)
    for place, (attention, unit) in enumerate(units):
        scores = ahead
        if place + 1 < len(units):
            ahead = units[place + 1][0].score(units[place + 1][1])
        attention.mix(unit, attention.weigh(unit, scores))
        if unit == attention.units - 1:
            finish(attentions.index(attention), attention.result())


def mask_columns(mask_row):
    shape = (128, mask_row.shape[1])
    top = lax.broadcasted_iota(jnp.int32, shape, 0) == 0
    return jnp.where(top, jnp.broadcast_to(mask_row, shape), 0.0).astype(BF16).T


def factor_kernel(x_ref, mask_ref, source_ref, target_ref, left_ref, right_ref, lefts, rights):
    ln = normalize(x_ref[...].reshape(1536, 256))
    mask = mask_ref[...].astype(F32).T
    lefts[:, :32] = lax.dot_general(ln, source_ref[...], NT, preferred_element_type=F32)
    turned = lax.dot_general(target_ref[...], ln, NT, preferred_element_type=F32)
    for s in range(48):
        rights[s * 32 : (s + 1) * 32, :32] = turned[:, s * 32 : (s + 1) * 32]
    wide = jnp.concatenate([mask] * 4, axis=1)
    for tile in range(8):
        lanes = slice(tile * 128, (tile + 1) * 128)
        spots = [pl.ds(tile * 4 + e, 48, stride=32) for e in range(4)]
        parts = [lefts[spot, :][:, :32] for spot in spots]
        parts = [p * mask[:, tile * 4 + e : tile * 4 + e + 1] for e, p in enumerate(parts)]
        left_ref[:, lanes] = jnp.concatenate(parts, axis=1).astype(BF16)
        parts = [rights[spot, :][:, :32] for spot in spots]
        right_ref[:, lanes] = (jnp.concatenate(parts, axis=1) * wide).astype(BF16)
    tail = jnp.concatenate([mask, jnp.zeros((48, 96), F32)], axis=1).astype(BF16)
    left_ref[:, 1024:] = tail
    right_ref[:, 1024:] = tail


def pair_kernel(at_ref, *refs):
    left_pieces = refs[:4]
    mine_ref, other_ref, pair_ref, rows_ref, cols_ref, final_ref, offset_ref = refs[4:11]
    out_ref, bias_ref, column_ref, left_hold, right_hold, hold = refs[11:]
    seq_at, core = at_ref[0], at_ref[1]
    for k in range(8):
        place = k // 4 * 4 + (k + 8 - seq_at) % 4
        right_hold[core, place] = mine_ref[k]
        right_hold[1 - core, place] = other_ref[k]
    for k in range(8):
        left_hold[seq_at ^ k] = left_pieces[k % 4][k // 4]
    left_all = left_hold[...].reshape(384, 1152)
    right = [right_hold[p].reshape(384, 1152) for p in range(2)]
    left_mask = left_all[:, 1024:1056]
    picks = lax.broadcasted_iota(jnp.int32, (8, 32), 0) + seq_at * 4
    picks = (picks == lax.broadcasted_iota(jnp.int32, (8, 32), 1)).astype(BF16)
    present = lax.dot_general(picks, left_mask, NT, preferred_element_type=F32)
    column_ref[...] = (present - 1.0) * -NEG
    count = jnp.concatenate(
        [
            lax.dot_general(r[:, 1024:1056], left_mask, TN, preferred_element_type=F32)
            for r in right
        ],
        axis=0,
    )
    factor = cols_ref[...] * rows_ref[...] / (count + 0.001)
    offset = offset_ref[...]
    def outer_of(block):
        left = left_all[:, block * 1024 : (block + 1) * 1024]
        return [
            lax.dot_general(left, r[:, :1024], TN, preferred_element_type=F32).astype(BF16)
            for r in right
        ]

    for block in range(1):
        outer = outer_of(block)
        turned = []
        for i in range(32):
            for p in range(2):
                rows = outer[p][i * 32 : (i + 1) * 32]
                tiles = [rows[:, t * 128 : (t + 1) * 128] for t in range(8)]
                turned.append(jnp.concatenate(tiles, axis=0).T)
        terms = None
        for e in range(4):
            lhs = jnp.concatenate([t[e * 32 : (e + 1) * 32] for t in turned], axis=0)
            part = project(lhs, final_ref[e])
            terms = part if terms is None else terms + part
        for i in range(32):
            at = block * 32 + i
            sums = terms[i * 64 : (i + 1) * 64]
            fresh = pair_ref[at].astype(F32) + factor[:, at : at + 1] * sums
            fresh = fresh.astype(BF16)
            out_ref[at] = fresh
            bias = lax.dot_general(offset, normalize(fresh), NT, preferred_element_type=F32)
            hold[:, at : at + 1, :] = bias[:, None, :]
    for h in range(8):
        turned = hold[h].T
        quarters = [turned[q * 16 : (q + 1) * 16] for q in range(4)]
        block = jnp.concatenate(quarters, axis=1).astype(BF16)
        for reader in range(32):
            bias_ref[reader, h] = block


def ready_kernel(at_ref, *refs):
    x_ref, xc_ref, xx_ref, xxc_ref = refs[:4]
    tails = refs[4:8]
    wq_ref, wk_ref, wv_ref, wg_ref = refs[8:12]
    query_ref, key_ref, value_ref, gate_ref, mask_ref, ordered, columns = refs[12:]
    xl, core = at_ref[0], at_ref[1]

    @pl.when(pl.program_id(0) == 0)
    def _():
        places = [(xl, core), (xl, 1 - core), (1 - xl, core), (1 - xl, 1 - core)]
        for tail_ref, (a, b) in zip(tails, places):
            columns[:, a, b] = (tail_ref[:, :, :128].astype(F32) - 1.0) * -NEG
        mask_ref[...] = columns[...].reshape(512, 128).astype(BF16)

    for t in range(STEP):
        rows = slice(t * 32, (t + 1) * 32)
        asked = normalize(x_ref[:, rows].reshape(128, 256))
        ordered[t, :, xl, core] = asked.reshape(4, 32, 256)
        ordered[t, :, xl, 1 - core] = normalize(xc_ref[:, rows])
        ordered[t, :, 1 - xl, core] = normalize(xx_ref[:, rows])
        ordered[t, :, 1 - xl, 1 - core] = normalize(xxc_ref[:, rows])
        keys = ordered[t].reshape(512, 256)
        query_ref[t] = (project(asked, wq_ref[...]) * (HEAD**-0.5 * LOG2E)).T.astype(BF16)
        key_ref[t] = project(keys, wk_ref[...]).astype(BF16)
        value_ref[t] = project(keys, wv_ref[...]).astype(BF16).T
        gate_ref[t] = jax.nn.sigmoid(project(asked, wg_ref[...])).T


def row_kernel(
    at_ref, x_ref, query_ref, key_ref, value_ref, gate_ref, mask_ref, bias_ref, wo_ref, out_ref, held
):
    @pl.when(pl.program_id(0) == 0)
    def _():
        for a in range(8):
            for j in range(4):
                low = a * 64 + j * 16
                parts = [bias_ref[a, q, :, :, j * 32 : (j + 1) * 32] for q in range(4)]
                part = jnp.concatenate(parts, axis=2).astype(F32)
                held[:, low : low + 16] = part * LOG2E

    def finish(t, found):
        gated = (gate_ref[t] * found).astype(BF16)
        update = lax.dot_general(gated, wo_ref[...], TN, preferred_element_type=F32).astype(BF16)
        raw = x_ref[:, t * 32 : (t + 1) * 32].reshape(128, 256)
        out_ref[t] = (raw.astype(F32) + update.astype(F32)).astype(BF16)

    attentions = [
        Attention(
            query_ref[t],
            key_ref[t],
            value_ref[t],
            lambda h: held[h],
            mask_ref[...],
            at_ref[0] * 12 + pl.program_id(0) * TURN + t,
            4,
        )
        for t in range(TURN)
    ]
    run_pipelined(attentions, finish)


def column_kernel(x_ref, mask_ref, wq_ref, wk_ref, wv_ref, wg_ref, wo_ref, out_ref):
    keys = normalize(x_ref[...].reshape(PICK * 384, 256))
    key = project(keys, wk_ref[...]).astype(BF16)
    weights = jnp.concatenate([wq_ref[...], wv_ref[...], wg_ref[...]], axis=1)
    turned = lax.dot_general(weights, keys.T, TN, preferred_element_type=F32)
    query_t = (turned[:256] * (HEAD**-0.5 * LOG2E)).astype(BF16)
    value_t = turned[256:512].astype(BF16)
    gate = jax.nn.sigmoid(turned[512:])
    gates, attentions = [], []
    for r in range(PICK):
        rows = slice(r * 384, (r + 1) * 384)
        gates.append(gate[:, rows])
        mask = mask_columns(mask_ref[pl.ds(pl.program_id(0) * PICK + r, 1), :])
        attentions.append(
            Attention(query_t[:, rows], key[rows], value_t[:, rows], lambda h: None, mask, 0, 2)
        )

    def finish(r, found):
        gated = (gates[r] * found).astype(BF16)
        update = lax.dot_general(gated, wo_ref[...], TN, preferred_element_type=F32).astype(BF16)
        out_ref[r] = (x_ref[r].astype(F32) + update.astype(F32)).astype(BF16)

    run_pipelined(attentions, finish)


def in_hbm(array):
    return pltpu.with_memory_space_constraint(array, pltpu.HBM)


def spread(block, axes, count):
    wide = jnp.broadcast_to(block[None], (count,) + block.shape)
    return lax.all_to_all(wide, axes, split_axis=0, concat_axis=0, tiled=True)


def whole(shape):
    zeros = (0,) * len(shape)
    return pl.BlockSpec(shape, lambda *_: zeros)


def body(
    homolog_stack,
    entry_exists_flags,
    genuine_amino_flags,
    couplings_tensor,
    product_source_weights,
    product_target_weights,
    product_final_weights,
    coupling_logit_offset,
    horizontal_asking_weights,
    horizontal_lookup_weights,
    horizontal_content_weights,
    horizontal_sigmoid_weights,
    horizontal_final_weights,
    vertical_asking_weights,
    vertical_lookup_weights,
    vertical_content_weights,
    vertical_sigmoid_weights,
    vertical_final_weights,
):
    seq_at = lax.axis_index(SEQ)
    res_at = lax.axis_index(RES)
    xl_at = lax.axis_index("xl")
    core_at = lax.axis_index("core")

    tail = jnp.pad(entry_exists_flags.T.astype(BF16), ((0, 0), (0, 208)))
    tail = jnp.broadcast_to(tail[None], (4, 32, 256))
    packed = jnp.concatenate([homolog_stack.reshape(4, 384, 256), tail], axis=1)
    team_at = lax.axis_index(TEAM)
    parts = []
    for k in range(4):
        part = lax.dynamic_index_in_dim(packed, team_at ^ k, 0, False)
        parts.append(lax.ppermute(part, TEAM, [(t, t ^ k) for t in range(4)]) if k else part)
    packed = jnp.stack(parts).reshape(2, 2, 416, 256)
    packed = jnp.where(lax.axis_index("yl") == 1, packed[::-1], packed)
    packed = jnp.where(lax.axis_index("xh") == 1, packed[:, ::-1], packed)
    packed = packed.reshape(4, 416, 256)

    left, right = pl.pallas_call(
        factor_kernel,
        out_shape=[jax.ShapeDtypeStruct((48, 1152), BF16)] * 2,
        scratch_shapes=[pltpu.VMEM((1536, 128), F32)] * 2,
        compiler_params=pltpu.CompilerParams(vmem_limit_bytes=VMEM_LIMIT),
        name="factors",
    )(
        in_hbm(homolog_stack),
        in_hbm(entry_exists_flags.T),
        in_hbm(product_source_weights.T),
        in_hbm(product_target_weights.T),
    )
    swap = [
        ((a * 8 + b) * 2 + p, (b * 8 + a // 4 * 4 + (a + b) % 4) * 2 + p)
        for a in range(8)
        for b in range(8)
        for p in range(2)
    ]
    pairs = [(0, 1), (1, 0)]
    right = lax.ppermute(right, ALL, swap)
    left_yh = lax.ppermute(left, "yh", pairs)
    right, left_yh, packed = lax.optimization_barrier((right, left_yh, packed))
    mine = spread(right, ("yl", "xh", "xl"), 8)
    left = jnp.stack([left, left_yh])
    lefts = [left] + [
        lax.ppermute(left, "z", [(z, z ^ k) for z in range(4)]) for k in range(1, 4)
    ]
    final = product_final_weights.reshape(32, 8, 4, 128)
    final = jnp.transpose(final, (2, 1, 0, 3)).reshape(4, 256, 128)
    mine, final, *lefts = lax.optimization_barrier((mine, final, *lefts))
    other = lax.ppermute(mine, "core", pairs)
    packed_x = lax.ppermute(packed, "xl", pairs)
    packed_c = lax.ppermute(packed, "core", pairs)

    flags = genuine_amino_flags.astype(F32)
    row_flags = lax.dynamic_slice_in_dim(flags, res_at * 32, 32).reshape(1, 32)
    col_flags = lax.dynamic_slice_in_dim(flags, seq_at * 64, 64).reshape(64, 1)
    square = whole((256, 256))
    smem = pl.BlockSpec(memory_space=pltpu.SMEM)
    vmem = pl.BlockSpec(memory_space=pltpu.VMEM)
    pair_output, bias, col_mask = pl.pallas_call(
        pair_kernel,
        out_shape=(
            jax.ShapeDtypeStruct((32, 64, 128), BF16),
            jax.ShapeDtypeStruct((32, 8, 16, 128), BF16),
            jax.ShapeDtypeStruct((8, 384), F32),
        ),
        in_specs=[smem] + [vmem] * 11,
        scratch_shapes=[
            pltpu.VMEM((8, 48, 1152), BF16),
            pltpu.VMEM((2, 8, 48, 1152), BF16),
            pltpu.VMEM((8, 32, 64), F32),
        ],
        compiler_params=pltpu.CompilerParams(vmem_limit_bytes=VMEM_LIMIT),
        cost_estimate=pl.CostEstimate(
            flops=1000, transcendentals=0, bytes_accessed=1000
        ),
        name="pair",
    )(
        jnp.stack([seq_at, core_at]).astype(jnp.int32),
        *lefts,
        mine,
        other,
        couplings_tensor,
        row_flags,
        col_flags,
        final,
        coupling_logit_offset.T,
    )

    packed, packed_c, packed_x, _ = lax.optimization_barrier((packed, packed_c, packed_x, bias))
    packed_xc = lax.ppermute(packed_x, "core", pairs)
    pieces = [in_hbm(p) for p in (packed, packed_c, packed_x)] + [packed_xc]
    by_row = [(12, 256, 128), (12, 512, 256), (12, 256, 512), (12, 256, 128)]
    specs = [pl.BlockSpec((STEP,) + shape[1:], lambda t: (t, 0, 0)) for shape in by_row]
    rows_in = pl.pallas_call(
        ready_kernel,
        out_shape=[
            pltpu.HBM(shape, kind)
            for shape, kind in zip(by_row, (BF16, BF16, BF16, F32))
        ]
        + [pltpu.HBM((512, 128), BF16)],
        grid=(12 // STEP,),
        in_specs=[smem] + [pl.BlockSpec((4, STEP * 32, 256), lambda t: (0, t, 0))] * 4
        + [pl.BlockSpec((4, 32, 256), lambda t: (0, 12, 0))] * 4
        + [square] * 4,
        out_specs=specs + [whole((512, 128))],
        scratch_shapes=[
            pltpu.VMEM((STEP, 4, 2, 2, 32, 256), BF16),
            pltpu.VMEM((4, 2, 2, 32, 128), F32),
        ],
        compiler_params=pltpu.CompilerParams(vmem_limit_bytes=VMEM_LIMIT),
        cost_estimate=pl.CostEstimate(flops=1000, transcendentals=0, bytes_accessed=1000),
        name="ready",
    )(
        jnp.stack([xl_at, core_at]).astype(jnp.int32),
        *pieces,
        *pieces,
        in_hbm(horizontal_asking_weights),
        in_hbm(horizontal_lookup_weights),
        in_hbm(horizontal_content_weights),
        in_hbm(horizontal_sigmoid_weights),
    )
    bias = lax.all_to_all(bias, PLANE, split_axis=0, concat_axis=0, tiled=True)
    bias = bias.reshape(8, 4, 8, 16, 128)

    rows_in = [in_hbm(a) for a in rows_in]
    middle = pl.pallas_call(
        row_kernel,
        out_shape=jax.ShapeDtypeStruct((12, 128, 256), BF16),
        grid=(12 // TURN,),
        in_specs=[smem, pl.BlockSpec((4, TURN * 32, 256), lambda t: (0, t, 0))]
        + [pl.BlockSpec((TURN,) + shape[1:], lambda t: (t, 0, 0)) for shape in by_row]
        + [whole((512, 128)), whole((8, 4, 8, 16, 128)), square],
        out_specs=pl.BlockSpec((TURN, 128, 256), lambda t: (t, 0, 0)),
        scratch_shapes=[pltpu.VMEM((8, 512, 128), F32)],
        compiler_params=pltpu.CompilerParams(vmem_limit_bytes=VMEM_LIMIT),
        cost_estimate=pl.CostEstimate(
            flops=8_000_000_000, transcendentals=6_300_000, bytes_accessed=12_000_000
        ),
        name="rows",
    )(team_at.astype(jnp.int32).reshape(1), pieces[0], *rows_in, bias, horizontal_final_weights)

    middle = jnp.transpose(middle.reshape(12, 4, 8, 4, 256), (2, 1, 0, 3, 4))
    middle = lax.all_to_all(
        middle.reshape(32, 12, 4, 256), PLANE, split_axis=0, concat_axis=0, tiled=True
    )
    middle = jnp.transpose(middle.reshape(384, 4, 256), (1, 0, 2))
    columns = pl.pallas_call(
        column_kernel,
        out_shape=jax.ShapeDtypeStruct((4, 384, 256), BF16),
        grid=(4 // PICK,),
        in_specs=[
            pl.BlockSpec((PICK, 384, 256), lambda r: (r, 0, 0)),
            whole((8, 384)),
            square,
            square,
            square,
            square,
            square,
        ],
        out_specs=pl.BlockSpec((PICK, 384, 256), lambda r: (r, 0, 0)),
        compiler_params=pltpu.CompilerParams(vmem_limit_bytes=VMEM_LIMIT),
        cost_estimate=pl.CostEstimate(
            flops=8_000_000_000, transcendentals=4_700_000, bytes_accessed=2_000_000
        ),
        name="columns",
    )(
        middle,
        col_mask,
        vertical_asking_weights,
        vertical_lookup_weights,
        vertical_content_weights,
        vertical_sigmoid_weights,
        vertical_final_weights,
    )
    columns = jnp.transpose(columns.reshape(4, 8, 48, 256), (1, 0, 2, 3))
    columns = lax.all_to_all(columns, SEQ, split_axis=0, concat_axis=0, tiled=True)
    alignment_output = jnp.transpose(columns.reshape(32, 48, 256), (1, 0, 2))
    return alignment_output, pair_output


def solution(mesh):
    parts = Mesh(mesh.devices.reshape(2, 4, 2, 2, 2, 2), ALL)
    stack = P(SEQ, RES, None)
    in_specs = (stack, P(SEQ, RES), P(), P(RES, SEQ, None)) + (P(),) * 14
    out_specs = (stack, P(RES, SEQ, None))
    return jax.shard_map(body, mesh=parts, in_specs=in_specs, out_specs=out_specs, check_vma=False)
```

```python
import math

import jax
import jax.numpy as jnp
from jax import lax
from jax.experimental import pallas as pl
from jax.experimental.pallas import tpu as pltpu
from jax.sharding import Mesh
from jax.sharding import PartitionSpec as P

HEADS = 8
HEAD = 32
F32 = jnp.float32
BF16 = jnp.bfloat16
NEG = -1e9
STEP = 3
TURN = 6
PICK = 4
SEQ = ("yh", "z")
RES = ("yl", "xh", "xl", "core")
ALL = SEQ + RES
TEAM = ("yl", "xh")
PLANE = SEQ + TEAM
NT = (((1,), (1,)), ((), ()))
TN = (((0,), (0,)), ((), ()))
VMEM_LIMIT = 28 * 1024 * 1024
LOG2E = math.log2(math.e)


def normalize(values):
    values = values.astype(F32)
    center = values - jnp.mean(values, axis=-1, keepdims=True)
    spread = jnp.mean(center * center, axis=-1, keepdims=True)
    return (center * lax.rsqrt(spread + 1e-5)).astype(BF16)


def project(values, weight):
    return jnp.dot(values, weight, preferred_element_type=F32)


class Attention:
    def __init__(self, query_t, key, value_t, bias_of, mask_lanes, lane, heads):
        self.query_t, self.key, self.value_t = query_t, key, value_t
        self.bias_of, self.mask_lanes, self.lane = bias_of, mask_lanes, lane
        self.heads = heads
        self.units = HEADS // heads
        self.count = query_t.shape[1]
        self.found = []

    def score(self, unit):
        first = unit * self.heads
        part = slice(first // 4 * 128, first // 4 * 128 + 128)
        own = self.query_t[part]
        row = lax.broadcasted_iota(jnp.int32, own.shape, 0)
        one = jnp.where(row == self.lane, 1.0, 0.0).astype(BF16)
        stacked = []
        for h in range(self.heads):
            mine = row // HEAD == first % 4 + h
            stacked.append(jnp.concatenate([jnp.where(mine, own, jnp.zeros_like(own)), one], axis=0))
        keys = jnp.concatenate([self.key[:, part], self.mask_lanes], axis=1)
        return project(keys, jnp.concatenate(stacked, axis=1))

    def weigh(self, unit, scores):
        weights = []
        for h in range(self.heads):
            extra = self.bias_of(unit * self.heads + h)
            for low in range(0, self.count, 128):
                tile = scores[:, h * self.count + low : h * self.count + low + 128]
                if extra is not None:
                    tile = tile + extra[:, low : low + 128]
                weights.append(jnp.exp2(tile - jnp.max(tile, axis=0, keepdims=True)).astype(BF16))
        return jnp.concatenate(weights, axis=1)

    def mix(self, unit, weights):
        size = self.heads * HEAD
        ones = jnp.ones((16, self.value_t.shape[1]), BF16)
        values = jnp.concatenate([self.value_t[unit * size : (unit + 1) * size], ones], axis=0)
        mixed = project(values, weights)
        for h in range(self.heads):
            cols = slice(h * self.count, (h + 1) * self.count)
            self.found.append(mixed[h * HEAD : (h + 1) * HEAD, cols] / mixed[size : size + 1, cols])

    def result(self):
        return jnp.concatenate(self.found, axis=0)


def run_pipelined(attentions, finish):
    units = [(a, unit) for a in attentions for unit in range(a.units)]

    def close(attention, unit, weights):
        attention.mix(unit, weights)
        if unit == attention.units - 1:
            finish(attentions.index(attention), attention.result())

    ahead = units[0][0].score(0)
    behind = None
    for place, (attention, unit) in enumerate(units):
        scores = ahead
        if place + 1 < len(units):
            ahead = units[place + 1][0].score(units[place + 1][1])
        if behind is not None:
            close(*behind)
        behind = (attention, unit, attention.weigh(unit, scores))
    close(*behind)


def mask_columns(mask_row):
    shape = (128, mask_row.shape[1])
    top = lax.broadcasted_iota(jnp.int32, shape, 0) == 0
    return jnp.where(top, jnp.broadcast_to(mask_row, shape), 0.0).astype(BF16).T


def factor_kernel(x_ref, mask_ref, source_ref, target_ref, left_ref, right_ref, lefts, rights):
    ln = normalize(x_ref[...].reshape(1536, 256))
    mask = mask_ref[...].astype(F32).T
    lefts[:, :32] = lax.dot_general(ln, source_ref[...], NT, preferred_element_type=F32)
    turned = lax.dot_general(target_ref[...], ln, NT, preferred_element_type=F32)
    for s in range(48):
        rights[s * 32 : (s + 1) * 32, :32] = turned[:, s * 32 : (s + 1) * 32]
    wide = jnp.concatenate([mask] * 4, axis=1)
    for tile in range(8):
        lanes = slice(tile * 128, (tile + 1) * 128)
        spots = [pl.ds(tile * 4 + e, 48, stride=32) for e in range(4)]
        parts = [lefts[spot, :][:, :32] for spot in spots]
        parts = [p * mask[:, tile * 4 + e : tile * 4 + e + 1] for e, p in enumerate(parts)]
        left_ref[:, lanes] = jnp.concatenate(parts, axis=1).astype(BF16)
        parts = [rights[spot, :][:, :32] for spot in spots]
        right_ref[:, lanes] = (jnp.concatenate(parts, axis=1) * wide).astype(BF16)
    tail = jnp.concatenate([mask, jnp.zeros((48, 96), F32)], axis=1).astype(BF16)
    left_ref[:, 1024:] = tail
    right_ref[:, 1024:] = tail


def pair_kernel(at_ref, *refs):
    left_pieces = refs[:4]
    mine_ref, other_ref, pair_ref, rows_ref, cols_ref, final_ref, offset_ref = refs[4:11]
    out_ref, bias_ref, column_ref, left_hold, right_hold, hold = refs[11:]
    seq_at, core = at_ref[0], at_ref[1]
    for k in range(8):
        place = k // 4 * 4 + (k + 8 - seq_at) % 4
        right_hold[core, place] = mine_ref[k]
        right_hold[1 - core, place] = other_ref[k]
    for k in range(8):
        left_hold[seq_at ^ k] = left_pieces[k % 4][k // 4]
    left_all = left_hold[...].reshape(384, 1152)
    right = [right_hold[p].reshape(384, 1152) for p in range(2)]
    left_mask = left_all[:, 1024:1056]
    picks = lax.broadcasted_iota(jnp.int32, (8, 32), 0) + seq_at * 4
    picks = (picks == lax.broadcasted_iota(jnp.int32, (8, 32), 1)).astype(BF16)
    present = lax.dot_general(picks, left_mask, NT, preferred_element_type=F32)
    column_ref[...] = (present - 1.0) * -NEG
    count = jnp.concatenate(
        [
            lax.dot_general(r[:, 1024:1056], left_mask, TN, preferred_element_type=F32)
            for r in right
        ],
        axis=0,
    )
    factor = cols_ref[...] * rows_ref[...] / (count + 0.001)
    offset = offset_ref[...]
    def outer_of(block):
        left = left_all[:, block * 1024 : (block + 1) * 1024]
        return [
            lax.dot_general(left, r[:, :1024], TN, preferred_element_type=F32).astype(BF16)
            for r in right
        ]

    for block in range(1):
        outer = outer_of(block)
        turned = []
        for i in range(32):
            for p in range(2):
                rows = outer[p][i * 32 : (i + 1) * 32]
                tiles = [rows[:, t * 128 : (t + 1) * 128] for t in range(8)]
                turned.append(jnp.concatenate(tiles, axis=0).T)
        terms = None
        for e in range(4):
            lhs = jnp.concatenate([t[e * 32 : (e + 1) * 32] for t in turned], axis=0)
            part = project(lhs, final_ref[e])
            terms = part if terms is None else terms + part
        for i in range(32):
            at = block * 32 + i
            sums = terms[i * 64 : (i + 1) * 64]
            fresh = pair_ref[at].astype(F32) + factor[:, at : at + 1] * sums
            fresh = fresh.astype(BF16)
            out_ref[at] = fresh
            bias = lax.dot_general(offset, normalize(fresh), NT, preferred_element_type=F32)
            hold[:, at : at + 1, :] = bias[:, None, :]
    for h in range(8):
        turned = hold[h].T
        quarters = [turned[q * 16 : (q + 1) * 16] for q in range(4)]
        block = jnp.concatenate(quarters, axis=1).astype(BF16)
        for reader in range(32):
            bias_ref[reader, h] = block


def ready_kernel(at_ref, *refs):
    x_ref, xc_ref, xx_ref, xxc_ref = refs[:4]
    tails = refs[4:8]
    wq_ref, wk_ref, wv_ref, wg_ref = refs[8:12]
    query_ref, key_ref, value_ref, gate_ref, mask_ref, ordered, columns = refs[12:]
    xl, core = at_ref[0], at_ref[1]

    @pl.when(pl.program_id(0) == 0)
    def _():
        places = [(xl, core), (xl, 1 - core), (1 - xl, core), (1 - xl, 1 - core)]
        for tail_ref, (a, b) in zip(tails, places):
            columns[:, a, b] = (tail_ref[:, :, :128].astype(F32) - 1.0) * -NEG
        mask_ref[...] = columns[...].reshape(512, 128).astype(BF16)

    for t in range(STEP):
        rows = slice(t * 32, (t + 1) * 32)
        asked = normalize(x_ref[:, rows].reshape(128, 256))
        ordered[t, :, xl, core] = asked.reshape(4, 32, 256)
        ordered[t, :, xl, 1 - core] = normalize(xc_ref[:, rows])
        ordered[t, :, 1 - xl, core] = normalize(xx_ref[:, rows])
        ordered[t, :, 1 - xl, 1 - core] = normalize(xxc_ref[:, rows])
        keys = ordered[t].reshape(512, 256)
        query_ref[t] = (project(asked, wq_ref[...]) * (HEAD**-0.5 * LOG2E)).T.astype(BF16)
        key_ref[t] = project(keys, wk_ref[...]).astype(BF16)
        value_ref[t] = project(keys, wv_ref[...]).astype(BF16).T
        gate_ref[t] = jax.nn.sigmoid(project(asked, wg_ref[...])).T


def row_kernel(
    at_ref, x_ref, query_ref, key_ref, value_ref, gate_ref, mask_ref, bias_ref, wo_ref, out_ref, held
):
    @pl.when(pl.program_id(0) == 0)
    def _():
        for a in range(8):
            for j in range(4):
                low = a * 64 + j * 16
                parts = [bias_ref[a, q, :, :, j * 32 : (j + 1) * 32] for q in range(4)]
                part = jnp.concatenate(parts, axis=2).astype(F32)
                held[:, low : low + 16] = part * LOG2E

    def finish(t, found):
        gated = (gate_ref[t] * found).astype(BF16)
        update = lax.dot_general(gated, wo_ref[...], TN, preferred_element_type=F32).astype(BF16)
        raw = x_ref[:, t * 32 : (t + 1) * 32].reshape(128, 256)
        out_ref[t] = (raw.astype(F32) + update.astype(F32)).astype(BF16)

    attentions = [
        Attention(
            query_ref[t],
            key_ref[t],
            value_ref[t],
            lambda h: held[h],
            mask_ref[...],
            at_ref[0] * 12 + pl.program_id(0) * TURN + t,
            4,
        )
        for t in range(TURN)
    ]
    run_pipelined(attentions, finish)


def column_kernel(x_ref, mask_ref, wq_ref, wk_ref, wv_ref, wg_ref, wo_ref, out_ref):
    keys = normalize(x_ref[...].reshape(PICK * 384, 256))
    key = project(keys, wk_ref[...]).astype(BF16)
    weights = jnp.concatenate([wq_ref[...], wv_ref[...], wg_ref[...]], axis=1)
    turned = lax.dot_general(weights, keys.T, TN, preferred_element_type=F32)
    query_t = (turned[:256] * (HEAD**-0.5 * LOG2E)).astype(BF16)
    value_t = turned[256:512].astype(BF16)
    gate = jax.nn.sigmoid(turned[512:])
    gates, attentions = [], []
    for r in range(PICK):
        rows = slice(r * 384, (r + 1) * 384)
        gates.append(gate[:, rows])
        mask = mask_columns(mask_ref[pl.ds(pl.program_id(0) * PICK + r, 1), :])
        attentions.append(
            Attention(query_t[:, rows], key[rows], value_t[:, rows], lambda h: None, mask, 0, 2)
        )

    def finish(r, found):
        gated = (gates[r] * found).astype(BF16)
        update = lax.dot_general(gated, wo_ref[...], TN, preferred_element_type=F32).astype(BF16)
        out_ref[r] = (x_ref[r].astype(F32) + update.astype(F32)).astype(BF16)

    run_pipelined(attentions, finish)


def in_hbm(array):
    return pltpu.with_memory_space_constraint(array, pltpu.HBM)


def spread(block, axes, count):
    wide = jnp.broadcast_to(block[None], (count,) + block.shape)
    return lax.all_to_all(wide, axes, split_axis=0, concat_axis=0, tiled=True)


def whole(shape):
    zeros = (0,) * len(shape)
    return pl.BlockSpec(shape, lambda *_: zeros)


def body(
    homolog_stack,
    entry_exists_flags,
    genuine_amino_flags,
    couplings_tensor,
    product_source_weights,
    product_target_weights,
    product_final_weights,
    coupling_logit_offset,
    horizontal_asking_weights,
    horizontal_lookup_weights,
    horizontal_content_weights,
    horizontal_sigmoid_weights,
    horizontal_final_weights,
    vertical_asking_weights,
    vertical_lookup_weights,
    vertical_content_weights,
    vertical_sigmoid_weights,
    vertical_final_weights,
):
    seq_at = lax.axis_index(SEQ)
    res_at = lax.axis_index(RES)
    xl_at = lax.axis_index("xl")
    core_at = lax.axis_index("core")

    tail = jnp.pad(entry_exists_flags.T.astype(BF16), ((0, 0), (0, 208)))
    tail = jnp.broadcast_to(tail[None], (4, 32, 256))
    packed = jnp.concatenate([homolog_stack.reshape(4, 384, 256), tail], axis=1)
    team_at = lax.axis_index(TEAM)
    parts = []
    for k in range(4):
        part = lax.dynamic_index_in_dim(packed, team_at ^ k, 0, False)
        parts.append(lax.ppermute(part, TEAM, [(t, t ^ k) for t in range(4)]) if k else part)
    packed = jnp.stack(parts).reshape(2, 2, 416, 256)
    packed = jnp.where(lax.axis_index("yl") == 1, packed[::-1], packed)
    packed = jnp.where(lax.axis_index("xh") == 1, packed[:, ::-1], packed)
    packed = packed.reshape(4, 416, 256)

    left, right = pl.pallas_call(
        factor_kernel,
        out_shape=[jax.ShapeDtypeStruct((48, 1152), BF16)] * 2,
        scratch_shapes=[pltpu.VMEM((1536, 128), F32)] * 2,
        compiler_params=pltpu.CompilerParams(vmem_limit_bytes=VMEM_LIMIT),
        name="factors",
    )(
        in_hbm(homolog_stack),
        in_hbm(entry_exists_flags.T),
        in_hbm(product_source_weights.T),
        in_hbm(product_target_weights.T),
    )
    swap = [
        ((a * 8 + b) * 2 + p, (b * 8 + a // 4 * 4 + (a + b) % 4) * 2 + p)
        for a in range(8)
        for b in range(8)
        for p in range(2)
    ]
    pairs = [(0, 1), (1, 0)]
    right = lax.ppermute(right, ALL, swap)
    left_yh = lax.ppermute(left, "yh", pairs)
    right, left_yh, packed = lax.optimization_barrier((right, left_yh, packed))
    mine = spread(right, ("yl", "xh", "xl"), 8)
    left = jnp.stack([left, left_yh])
    lefts = [left] + [
        lax.ppermute(left, "z", [(z, z ^ k) for z in range(4)]) for k in range(1, 4)
    ]
    final = product_final_weights.reshape(32, 8, 4, 128)
    final = jnp.transpose(final, (2, 1, 0, 3)).reshape(4, 256, 128)
    mine, final, *lefts = lax.optimization_barrier((mine, final, *lefts))
    other = lax.ppermute(mine, "core", pairs)
    packed_x = lax.ppermute(packed, "xl", pairs)
    packed_c = lax.ppermute(packed, "core", pairs)

    flags = genuine_amino_flags.astype(F32)
    row_flags = lax.dynamic_slice_in_dim(flags, res_at * 32, 32).reshape(1, 32)
    col_flags = lax.dynamic_slice_in_dim(flags, seq_at * 64, 64).reshape(64, 1)
    square = whole((256, 256))
    smem = pl.BlockSpec(memory_space=pltpu.SMEM)
    vmem = pl.BlockSpec(memory_space=pltpu.VMEM)
    pair_output, bias, col_mask = pl.pallas_call(
        pair_kernel,
        out_shape=(
            jax.ShapeDtypeStruct((32, 64, 128), BF16),
            jax.ShapeDtypeStruct((32, 8, 16, 128), BF16),
            jax.ShapeDtypeStruct((8, 384), F32),
        ),
        in_specs=[smem] + [vmem] * 11,
        scratch_shapes=[
            pltpu.VMEM((8, 48, 1152), BF16),
            pltpu.VMEM((2, 8, 48, 1152), BF16),
            pltpu.VMEM((8, 32, 64), F32),
        ],
        compiler_params=pltpu.CompilerParams(vmem_limit_bytes=VMEM_LIMIT),
        cost_estimate=pl.CostEstimate(
            flops=1000, transcendentals=0, bytes_accessed=1000
        ),
        name="pair",
    )(
        jnp.stack([seq_at, core_at]).astype(jnp.int32),
        *lefts,
        mine,
        other,
        couplings_tensor,
        row_flags,
        col_flags,
        final,
        coupling_logit_offset.T,
    )

    packed, packed_c, packed_x, _ = lax.optimization_barrier((packed, packed_c, packed_x, bias))
    packed_xc = lax.ppermute(packed_x, "core", pairs)
    pieces = [in_hbm(p) for p in (packed, packed_c, packed_x)] + [packed_xc]
    by_row = [(12, 256, 128), (12, 512, 256), (12, 256, 512), (12, 256, 128)]
    specs = [pl.BlockSpec((STEP,) + shape[1:], lambda t: (t, 0, 0)) for shape in by_row]
    rows_in = pl.pallas_call(
        ready_kernel,
        out_shape=[
            pltpu.HBM(shape, kind)
            for shape, kind in zip(by_row, (BF16, BF16, BF16, F32))
        ]
        + [pltpu.HBM((512, 128), BF16)],
        grid=(12 // STEP,),
        in_specs=[smem] + [pl.BlockSpec((4, STEP * 32, 256), lambda t: (0, t, 0))] * 4
        + [pl.BlockSpec((4, 32, 256), lambda t: (0, 12, 0))] * 4
        + [square] * 4,
        out_specs=specs + [whole((512, 128))],
        scratch_shapes=[
            pltpu.VMEM((STEP, 4, 2, 2, 32, 256), BF16),
            pltpu.VMEM((4, 2, 2, 32, 128), F32),
        ],
        compiler_params=pltpu.CompilerParams(vmem_limit_bytes=VMEM_LIMIT),
        cost_estimate=pl.CostEstimate(flops=1000, transcendentals=0, bytes_accessed=1000),
        name="ready",
    )(
        jnp.stack([xl_at, core_at]).astype(jnp.int32),
        *pieces,
        *pieces,
        in_hbm(horizontal_asking_weights),
        in_hbm(horizontal_lookup_weights),
        in_hbm(horizontal_content_weights),
        in_hbm(horizontal_sigmoid_weights),
    )
    bias = lax.all_to_all(bias, PLANE, split_axis=0, concat_axis=0, tiled=True)
    bias = bias.reshape(8, 4, 8, 16, 128)

    rows_in = [in_hbm(a) for a in rows_in]
    middle = pl.pallas_call(
        row_kernel,
        out_shape=jax.ShapeDtypeStruct((12, 128, 256), BF16),
        grid=(12 // TURN,),
        in_specs=[smem, pl.BlockSpec((4, TURN * 32, 256), lambda t: (0, t, 0))]
        + [pl.BlockSpec((TURN,) + shape[1:], lambda t: (t, 0, 0)) for shape in by_row]
        + [whole((512, 128)), whole((8, 4, 8, 16, 128)), square],
        out_specs=pl.BlockSpec((TURN, 128, 256), lambda t: (t, 0, 0)),
        scratch_shapes=[pltpu.VMEM((8, 512, 128), F32)],
        compiler_params=pltpu.CompilerParams(vmem_limit_bytes=VMEM_LIMIT),
        cost_estimate=pl.CostEstimate(
            flops=8_000_000_000, transcendentals=6_300_000, bytes_accessed=12_000_000
        ),
        name="rows",
    )(team_at.astype(jnp.int32).reshape(1), pieces[0], *rows_in, bias, horizontal_final_weights)

    middle = jnp.transpose(middle.reshape(12, 4, 8, 4, 256), (2, 1, 0, 3, 4))
    middle = lax.all_to_all(
        middle.reshape(32, 12, 4, 256), PLANE, split_axis=0, concat_axis=0, tiled=True
    )
    middle = jnp.transpose(middle.reshape(384, 4, 256), (1, 0, 2))
    columns = pl.pallas_call(
        column_kernel,
        out_shape=jax.ShapeDtypeStruct((4, 384, 256), BF16),
        grid=(4 // PICK,),
        in_specs=[
            pl.BlockSpec((PICK, 384, 256), lambda r: (r, 0, 0)),
            whole((8, 384)),
            square,
            square,
            square,
            square,
            square,
        ],
        out_specs=pl.BlockSpec((PICK, 384, 256), lambda r: (r, 0, 0)),
        compiler_params=pltpu.CompilerParams(vmem_limit_bytes=VMEM_LIMIT),
        cost_estimate=pl.CostEstimate(
            flops=8_000_000_000, transcendentals=4_700_000, bytes_accessed=2_000_000
        ),
        name="columns",
    )(
        middle,
        col_mask,
        vertical_asking_weights,
        vertical_lookup_weights,
        vertical_content_weights,
        vertical_sigmoid_weights,
        vertical_final_weights,
    )
    columns = jnp.transpose(columns.reshape(4, 8, 48, 256), (1, 0, 2, 3))
    columns = lax.all_to_all(columns, SEQ, split_axis=0, concat_axis=0, tiled=True)
    alignment_output = jnp.transpose(columns.reshape(32, 48, 256), (1, 0, 2))
    return alignment_output, pair_output


def solution(mesh):
    parts = Mesh(mesh.devices.reshape(2, 4, 2, 2, 2, 2), ALL)
    stack = P(SEQ, RES, None)
    in_specs = (stack, P(SEQ, RES), P(), P(RES, SEQ, None)) + (P(),) * 14
    out_specs = (stack, P(RES, SEQ, None))
    return jax.shard_map(body, mesh=parts, in_specs=in_specs, out_specs=out_specs, check_vma=False)
```

```python
import math

import jax
import jax.numpy as jnp
from jax import lax
from jax.experimental import pallas as pl
from jax.experimental.pallas import tpu as pltpu
from jax.sharding import Mesh
from jax.sharding import PartitionSpec as P

HEADS = 8
HEAD = 32
F32 = jnp.float32
BF16 = jnp.bfloat16
NEG = -1e9
STEP = 6
TURN = 6
PICK = 4
SEQ = ("yh", "z")
RES = ("yl", "xh", "xl", "core")
ALL = SEQ + RES
TEAM = ("yl", "xh")
PLANE = SEQ + TEAM
NT = (((1,), (1,)), ((), ()))
TN = (((0,), (0,)), ((), ()))
VMEM_LIMIT = 28 * 1024 * 1024
LOG2E = math.log2(math.e)


def normalize(values):
    values = values.astype(F32)
    center = values - jnp.mean(values, axis=-1, keepdims=True)
    spread = jnp.mean(center * center, axis=-1, keepdims=True)
    return (center * lax.rsqrt(spread + 1e-5)).astype(BF16)


def project(values, weight):
    return jnp.dot(values, weight, preferred_element_type=F32)


class Attention:
    def __init__(self, query_t, key, value_t, bias_of, mask_lanes, lane, heads):
        self.query_t, self.key, self.value_t = query_t, key, value_t
        self.bias_of, self.mask_lanes, self.lane = bias_of, mask_lanes, lane
        self.heads = heads
        self.units = HEADS // heads
        self.count = query_t.shape[1]
        self.found = []

    def score(self, unit):
        first = unit * self.heads
        part = slice(first // 4 * 128, first // 4 * 128 + 128)
        own = self.query_t[part]
        row = lax.broadcasted_iota(jnp.int32, own.shape, 0)
        one = jnp.where(row == self.lane, 1.0, 0.0).astype(BF16)
        stacked = []
        for h in range(self.heads):
            mine = row // HEAD == first % 4 + h
            stacked.append(jnp.concatenate([jnp.where(mine, own, jnp.zeros_like(own)), one], axis=0))
        keys = jnp.concatenate([self.key[:, part], self.mask_lanes], axis=1)
        return project(keys, jnp.concatenate(stacked, axis=1))

    def weigh(self, unit, scores):
        weights = []
        for h in range(self.heads):
            extra = self.bias_of(unit * self.heads + h)
            for low in range(0, self.count, 128):
                tile = scores[:, h * self.count + low : h * self.count + low + 128]
                if extra is not None:
                    tile = tile + extra[:, low : low + 128]
                weights.append(jnp.exp2(tile - jnp.max(tile, axis=0, keepdims=True)).astype(BF16))
        return jnp.concatenate(weights, axis=1)

    def mix(self, unit, weights):
        size = self.heads * HEAD
        ones = jnp.ones((16, self.value_t.shape[1]), BF16)
        values = jnp.concatenate([self.value_t[unit * size : (unit + 1) * size], ones], axis=0)
        mixed = project(values, weights)
        for h in range(self.heads):
            cols = slice(h * self.count, (h + 1) * self.count)
            self.found.append(mixed[h * HEAD : (h + 1) * HEAD, cols] / mixed[size : size + 1, cols])

    def result(self):
        return jnp.concatenate(self.found, axis=0)


def run_pipelined(attentions, finish):
    units = [(a, unit) for a in attentions for unit in range(a.units)]
    ahead = units[0][0].score(0)
    for place, (attention, unit) in enumerate(units):
        scores = ahead
        if place + 1 < len(units):
            ahead = units[place + 1][0].score(units[place + 1][1])
        attention.mix(unit, attention.weigh(unit, scores))
        if unit == attention.units - 1:
            finish(attentions.index(attention), attention.result())


def mask_columns(mask_row):
    shape = (128, mask_row.shape[1])
    top = lax.broadcasted_iota(jnp.int32, shape, 0) == 0
    return jnp.where(top, jnp.broadcast_to(mask_row, shape), 0.0).astype(BF16).T


def factor_kernel(x_ref, mask_ref, source_ref, target_ref, left_ref, right_ref, lefts, rights):
    ln = normalize(x_ref[...].reshape(1536, 256))
    mask = mask_ref[...].astype(F32).T
    lefts[:, :32] = lax.dot_general(ln, source_ref[...], NT, preferred_element_type=F32)
    turned = lax.dot_general(target_ref[...], ln, NT, preferred_element_type=F32)
    for s in range(48):
        rights[s * 32 : (s + 1) * 32, :32] = turned[:, s * 32 : (s + 1) * 32]
    wide = jnp.concatenate([mask] * 4, axis=1)
    for tile in range(8):
        lanes = slice(tile * 128, (tile + 1) * 128)
        spots = [pl.ds(tile * 4 + e, 48, stride=32) for e in range(4)]
        parts = [lefts[spot, :][:, :32] for spot in spots]
        parts = [p * mask[:, tile * 4 + e : tile * 4 + e + 1] for e, p in enumerate(parts)]
        left_ref[:, lanes] = jnp.concatenate(parts, axis=1).astype(BF16)
        parts = [rights[spot, :][:, :32] for spot in spots]
        right_ref[:, lanes] = (jnp.concatenate(parts, axis=1) * wide).astype(BF16)
    tail = jnp.concatenate([mask, jnp.zeros((48, 96), F32)], axis=1).astype(BF16)
    left_ref[:, 1024:] = tail
    right_ref[:, 1024:] = tail


def pair_kernel(at_ref, *refs):
    left_pieces = refs[:4]
    mine_ref, other_ref, pair_ref, rows_ref, cols_ref, final_ref, offset_ref = refs[4:11]
    out_ref, bias_ref, column_ref, left_hold, right_hold, hold = refs[11:]
    seq_at, core = at_ref[0], at_ref[1]
    for k in range(8):
        place = k // 4 * 4 + (k + 8 - seq_at) % 4
        right_hold[core, place] = mine_ref[k]
        right_hold[1 - core, place] = other_ref[k]
    for k in range(8):
        left_hold[seq_at ^ k] = left_pieces[k % 4][k // 4]
    left_all = left_hold[...].reshape(384, 1152)
    right = [right_hold[p].reshape(384, 1152) for p in range(2)]
    left_mask = left_all[:, 1024:1056]
    picks = lax.broadcasted_iota(jnp.int32, (8, 32), 0) + seq_at * 4
    picks = (picks == lax.broadcasted_iota(jnp.int32, (8, 32), 1)).astype(BF16)
    present = lax.dot_general(picks, left_mask, NT, preferred_element_type=F32)
    column_ref[...] = (present - 1.0) * -NEG
    count = jnp.concatenate(
        [
            lax.dot_general(r[:, 1024:1056], left_mask, TN, preferred_element_type=F32)
            for r in right
        ],
        axis=0,
    )
    factor = cols_ref[...] * rows_ref[...] / (count + 0.001)
    offset = offset_ref[...]
    def outer_of(block):
        left = left_all[:, block * 1024 : (block + 1) * 1024]
        return [
            lax.dot_general(left, r[:, :1024], TN, preferred_element_type=F32).astype(BF16)
            for r in right
        ]

    for block in range(1):
        outer = outer_of(block)
        turned = []
        for i in range(32):
            for p in range(2):
                rows = outer[p][i * 32 : (i + 1) * 32]
                tiles = [rows[:, t * 128 : (t + 1) * 128] for t in range(8)]
                turned.append(jnp.concatenate(tiles, axis=0).T)
        terms = None
        for e in range(4):
            lhs = jnp.concatenate([t[e * 32 : (e + 1) * 32] for t in turned], axis=0)
            part = project(lhs, final_ref[e])
            terms = part if terms is None else terms + part
        for i in range(32):
            at = block * 32 + i
            sums = terms[i * 64 : (i + 1) * 64]
            fresh = pair_ref[at].astype(F32) + factor[:, at : at + 1] * sums
            fresh = fresh.astype(BF16)
            out_ref[at] = fresh
            bias = lax.dot_general(offset, normalize(fresh), NT, preferred_element_type=F32)
            hold[:, at : at + 1, :] = bias[:, None, :]
    for h in range(8):
        turned = hold[h].T
        quarters = [turned[q * 16 : (q + 1) * 16] for q in range(4)]
        block = jnp.concatenate(quarters, axis=1).astype(BF16)
        for reader in range(32):
            bias_ref[reader, h] = block


def ready_kernel(at_ref, *refs):
    x_ref, xc_ref, xx_ref, xxc_ref = refs[:4]
    tails = refs[4:8]
    wq_ref, wk_ref, wv_ref, wg_ref = refs[8:12]
    query_ref, key_ref, value_ref, gate_ref, mask_ref, ordered, columns = refs[12:]
    xl, core = at_ref[0], at_ref[1]

    @pl.when(pl.program_id(0) == 0)
    def _():
        places = [(xl, core), (xl, 1 - core), (1 - xl, core), (1 - xl, 1 - core)]
        for tail_ref, (a, b) in zip(tails, places):
            columns[:, a, b] = (tail_ref[:, :, :128].astype(F32) - 1.0) * -NEG
        mask_ref[...] = columns[...].reshape(512, 128).astype(BF16)

    for t in range(STEP):
        rows = slice(t * 32, (t + 1) * 32)
        asked = normalize(x_ref[:, rows].reshape(128, 256))
        ordered[t, :, xl, core] = asked.reshape(4, 32, 256)
        ordered[t, :, xl, 1 - core] = normalize(xc_ref[:, rows])
        ordered[t, :, 1 - xl, core] = normalize(xx_ref[:, rows])
        ordered[t, :, 1 - xl, 1 - core] = normalize(xxc_ref[:, rows])
        keys = ordered[t].reshape(512, 256)
        query_ref[t] = (project(asked, wq_ref[...]) * (HEAD**-0.5 * LOG2E)).T.astype(BF16)
        key_ref[t] = project(keys, wk_ref[...]).astype(BF16)
        value_ref[t] = project(keys, wv_ref[...]).astype(BF16).T
        gate_ref[t] = jax.nn.sigmoid(project(asked, wg_ref[...])).T


def row_kernel(
    at_ref, x_ref, query_ref, key_ref, value_ref, gate_ref, mask_ref, bias_ref, wo_ref, out_ref, held
):
    @pl.when(pl.program_id(0) == 0)
    def _():
        for a in range(8):
            for j in range(4):
                low = a * 64 + j * 16
                parts = [bias_ref[a, q, :, :, j * 32 : (j + 1) * 32] for q in range(4)]
                part = jnp.concatenate(parts, axis=2).astype(F32)
                held[:, low : low + 16] = part * LOG2E

    def finish(t, found):
        gated = (gate_ref[t] * found).astype(BF16)
        update = lax.dot_general(gated, wo_ref[...], TN, preferred_element_type=F32).astype(BF16)
        raw = x_ref[:, t * 32 : (t + 1) * 32].reshape(128, 256)
        out_ref[t] = (raw.astype(F32) + update.astype(F32)).astype(BF16)

    attentions = [
        Attention(
            query_ref[t],
            key_ref[t],
            value_ref[t],
            lambda h: held[h],
            mask_ref[...],
            at_ref[0] * 12 + pl.program_id(0) * TURN + t,
            4,
        )
        for t in range(TURN)
    ]
    run_pipelined(attentions, finish)


def column_kernel(x_ref, mask_ref, wq_ref, wk_ref, wv_ref, wg_ref, wo_ref, out_ref):
    keys = normalize(x_ref[...].reshape(PICK * 384, 256))
    key = project(keys, wk_ref[...]).astype(BF16)
    weights = jnp.concatenate([wq_ref[...], wv_ref[...], wg_ref[...]], axis=1)
    turned = lax.dot_general(weights, keys.T, TN, preferred_element_type=F32)
    query_t = (turned[:256] * (HEAD**-0.5 * LOG2E)).astype(BF16)
    value_t = turned[256:512].astype(BF16)
    gate = jax.nn.sigmoid(turned[512:])
    gates, attentions = [], []
    for r in range(PICK):
        rows = slice(r * 384, (r + 1) * 384)
        gates.append(gate[:, rows])
        mask = mask_columns(mask_ref[pl.ds(pl.program_id(0) * PICK + r, 1), :])
        attentions.append(
            Attention(query_t[:, rows], key[rows], value_t[:, rows], lambda h: None, mask, 0, 2)
        )

    def finish(r, found):
        gated = (gates[r] * found).astype(BF16)
        update = lax.dot_general(gated, wo_ref[...], TN, preferred_element_type=F32).astype(BF16)
        out_ref[r] = (x_ref[r].astype(F32) + update.astype(F32)).astype(BF16)

    run_pipelined(attentions, finish)


def in_hbm(array):
    return pltpu.with_memory_space_constraint(array, pltpu.HBM)


def spread(block, axes, count):
    wide = jnp.broadcast_to(block[None], (count,) + block.shape)
    return lax.all_to_all(wide, axes, split_axis=0, concat_axis=0, tiled=True)


def whole(shape):
    zeros = (0,) * len(shape)
    return pl.BlockSpec(shape, lambda *_: zeros)


def body(
    homolog_stack,
    entry_exists_flags,
    genuine_amino_flags,
    couplings_tensor,
    product_source_weights,
    product_target_weights,
    product_final_weights,
    coupling_logit_offset,
    horizontal_asking_weights,
    horizontal_lookup_weights,
    horizontal_content_weights,
    horizontal_sigmoid_weights,
    horizontal_final_weights,
    vertical_asking_weights,
    vertical_lookup_weights,
    vertical_content_weights,
    vertical_sigmoid_weights,
    vertical_final_weights,
):
    seq_at = lax.axis_index(SEQ)
    res_at = lax.axis_index(RES)
    xl_at = lax.axis_index("xl")
    core_at = lax.axis_index("core")

    tail = jnp.pad(entry_exists_flags.T.astype(BF16), ((0, 0), (0, 208)))
    tail = jnp.broadcast_to(tail[None], (4, 32, 256))
    packed = jnp.concatenate([homolog_stack.reshape(4, 384, 256), tail], axis=1)
    team_at = lax.axis_index(TEAM)
    parts = []
    for k in range(4):
        part = lax.dynamic_index_in_dim(packed, team_at ^ k, 0, False)
        parts.append(lax.ppermute(part, TEAM, [(t, t ^ k) for t in range(4)]) if k else part)
    packed = jnp.stack(parts).reshape(2, 2, 416, 256)
    packed = jnp.where(lax.axis_index("yl") == 1, packed[::-1], packed)
    packed = jnp.where(lax.axis_index("xh") == 1, packed[:, ::-1], packed)
    packed = packed.reshape(4, 416, 256)

    left, right = pl.pallas_call(
        factor_kernel,
        out_shape=[jax.ShapeDtypeStruct((48, 1152), BF16)] * 2,
        scratch_shapes=[pltpu.VMEM((1536, 128), F32)] * 2,
        compiler_params=pltpu.CompilerParams(vmem_limit_bytes=VMEM_LIMIT),
        name="factors",
    )(
        in_hbm(homolog_stack),
        in_hbm(entry_exists_flags.T),
        in_hbm(product_source_weights.T),
        in_hbm(product_target_weights.T),
    )
    swap = [
        ((a * 8 + b) * 2 + p, (b * 8 + a // 4 * 4 + (a + b) % 4) * 2 + p)
        for a in range(8)
        for b in range(8)
        for p in range(2)
    ]
    pairs = [(0, 1), (1, 0)]
    right = lax.ppermute(right, ALL, swap)
    left_yh = lax.ppermute(left, "yh", pairs)
    right, left_yh, packed = lax.optimization_barrier((right, left_yh, packed))
    mine = spread(right, ("yl", "xh", "xl"), 8)
    left = jnp.stack([left, left_yh])
    lefts = [left] + [
        lax.ppermute(left, "z", [(z, z ^ k) for z in range(4)]) for k in range(1, 4)
    ]
    final = product_final_weights.reshape(32, 8, 4, 128)
    final = jnp.transpose(final, (2, 1, 0, 3)).reshape(4, 256, 128)
    mine, final, *lefts = lax.optimization_barrier((mine, final, *lefts))
    other = lax.ppermute(mine, "core", pairs)
    packed_x = lax.ppermute(packed, "xl", pairs)
    packed_c = lax.ppermute(packed, "core", pairs)

    flags = genuine_amino_flags.astype(F32)
    row_flags = lax.dynamic_slice_in_dim(flags, res_at * 32, 32).reshape(1, 32)
    col_flags = lax.dynamic_slice_in_dim(flags, seq_at * 64, 64).reshape(64, 1)
    square = whole((256, 256))
    smem = pl.BlockSpec(memory_space=pltpu.SMEM)
    vmem = pl.BlockSpec(memory_space=pltpu.VMEM)
    pair_output, bias, col_mask = pl.pallas_call(
        pair_kernel,
        out_shape=(
            jax.ShapeDtypeStruct((32, 64, 128), BF16),
            jax.ShapeDtypeStruct((32, 8, 16, 128), BF16),
            jax.ShapeDtypeStruct((8, 384), F32),
        ),
        in_specs=[smem] + [vmem] * 11,
        scratch_shapes=[
            pltpu.VMEM((8, 48, 1152), BF16),
            pltpu.VMEM((2, 8, 48, 1152), BF16),
            pltpu.VMEM((8, 32, 64), F32),
        ],
        compiler_params=pltpu.CompilerParams(vmem_limit_bytes=VMEM_LIMIT),
        cost_estimate=pl.CostEstimate(
            flops=1000, transcendentals=0, bytes_accessed=1000
        ),
        name="pair",
    )(
        jnp.stack([seq_at, core_at]).astype(jnp.int32),
        *lefts,
        mine,
        other,
        couplings_tensor,
        row_flags,
        col_flags,
        final,
        coupling_logit_offset.T,
    )

    packed, packed_c, packed_x, _ = lax.optimization_barrier((packed, packed_c, packed_x, bias))
    packed_xc = lax.ppermute(packed_x, "core", pairs)
    pieces = [in_hbm(p) for p in (packed, packed_c, packed_x)] + [packed_xc]
    by_row = [(12, 256, 128), (12, 512, 256), (12, 256, 512), (12, 256, 128)]
    specs = [pl.BlockSpec((STEP,) + shape[1:], lambda t: (t, 0, 0)) for shape in by_row]
    rows_in = pl.pallas_call(
        ready_kernel,
        out_shape=[
            pltpu.HBM(shape, kind)
            for shape, kind in zip(by_row, (BF16, BF16, BF16, F32))
        ]
        + [pltpu.HBM((512, 128), BF16)],
        grid=(12 // STEP,),
        in_specs=[smem] + [pl.BlockSpec((4, STEP * 32, 256), lambda t: (0, t, 0))] * 4
        + [pl.BlockSpec((4, 32, 256), lambda t: (0, 12, 0))] * 4
        + [square] * 4,
        out_specs=specs + [whole((512, 128))],
        scratch_shapes=[
            pltpu.VMEM((STEP, 4, 2, 2, 32, 256), BF16),
            pltpu.VMEM((4, 2, 2, 32, 128), F32),
        ],
        compiler_params=pltpu.CompilerParams(vmem_limit_bytes=VMEM_LIMIT),
        cost_estimate=pl.CostEstimate(flops=1000, transcendentals=0, bytes_accessed=1000),
        name="ready",
    )(
        jnp.stack([xl_at, core_at]).astype(jnp.int32),
        *pieces,
        *pieces,
        in_hbm(horizontal_asking_weights),
        in_hbm(horizontal_lookup_weights),
        in_hbm(horizontal_content_weights),
        in_hbm(horizontal_sigmoid_weights),
    )
    bias = lax.all_to_all(bias, PLANE, split_axis=0, concat_axis=0, tiled=True)
    bias = bias.reshape(8, 4, 8, 16, 128)

    rows_in = [in_hbm(a) for a in rows_in]
    middle = pl.pallas_call(
        row_kernel,
        out_shape=jax.ShapeDtypeStruct((12, 128, 256), BF16),
        grid=(12 // TURN,),
        in_specs=[smem, pl.BlockSpec((4, TURN * 32, 256), lambda t: (0, t, 0))]
        + [pl.BlockSpec((TURN,) + shape[1:], lambda t: (t, 0, 0)) for shape in by_row]
        + [whole((512, 128)), whole((8, 4, 8, 16, 128)), square],
        out_specs=pl.BlockSpec((TURN, 128, 256), lambda t: (t, 0, 0)),
        scratch_shapes=[pltpu.VMEM((8, 512, 128), F32)],
        compiler_params=pltpu.CompilerParams(vmem_limit_bytes=VMEM_LIMIT),
        cost_estimate=pl.CostEstimate(
            flops=8_000_000_000, transcendentals=6_300_000, bytes_accessed=12_000_000
        ),
        name="rows",
    )(team_at.astype(jnp.int32).reshape(1), pieces[0], *rows_in, bias, horizontal_final_weights)

    middle = jnp.transpose(middle.reshape(12, 4, 8, 4, 256), (2, 1, 0, 3, 4))
    middle = lax.all_to_all(
        middle.reshape(32, 12, 4, 256), PLANE, split_axis=0, concat_axis=0, tiled=True
    )
    middle = jnp.transpose(middle.reshape(384, 4, 256), (1, 0, 2))
    columns = pl.pallas_call(
        column_kernel,
        out_shape=jax.ShapeDtypeStruct((4, 384, 256), BF16),
        grid=(4 // PICK,),
        in_specs=[
            pl.BlockSpec((PICK, 384, 256), lambda r: (r, 0, 0)),
            whole((8, 384)),
            square,
            square,
            square,
            square,
            square,
        ],
        out_specs=pl.BlockSpec((PICK, 384, 256), lambda r: (r, 0, 0)),
        compiler_params=pltpu.CompilerParams(vmem_limit_bytes=VMEM_LIMIT),
        cost_estimate=pl.CostEstimate(
            flops=8_000_000_000, transcendentals=4_700_000, bytes_accessed=2_000_000
        ),
        name="columns",
    )(
        middle,
        col_mask,
        vertical_asking_weights,
        vertical_lookup_weights,
        vertical_content_weights,
        vertical_sigmoid_weights,
        vertical_final_weights,
    )
    columns = jnp.transpose(columns.reshape(4, 8, 48, 256), (1, 0, 2, 3))
    columns = lax.all_to_all(columns, SEQ, split_axis=0, concat_axis=0, tiled=True)
    alignment_output = jnp.transpose(columns.reshape(32, 48, 256), (1, 0, 2))
    return alignment_output, pair_output


def solution(mesh):
    parts = Mesh(mesh.devices.reshape(2, 4, 2, 2, 2, 2), ALL)
    stack = P(SEQ, RES, None)
    in_specs = (stack, P(SEQ, RES), P(), P(RES, SEQ, None)) + (P(),) * 14
    out_specs = (stack, P(RES, SEQ, None))
    return jax.shard_map(body, mesh=parts, in_specs=in_specs, out_specs=out_specs, check_vma=False)
```
